32 devices in a mesh: batch: 8 (over z, y), seq: 4 (over x, core).
Axes of the slice: x: 2, y: 2, z: 4, core: 2. Of those that a mesh axis runs over, the one named last changes fastest.
Arguments:
- inputs: bfloat16 [64, 512, 768], P('batch', 'seq'), may hold values from -6 to 6
- out_grad: bfloat16 [64, 512, 768], P('batch', 'seq'), may hold values from -6 to 6
- lengths: int32 [64], P('batch'), may hold values from 128 to 512, as said below
- word_spans: int32 [64, 32, 2], P('batch'), may hold values from 0 to 511, as said below
- qkv_weight: float32 [1769472], P(('batch', 'seq')), may hold values from -0.21875 to 0.21875
- qkv_first: float32 [1769472], P(('batch', 'seq')), may hold values from -10 to 10
- qkv_second: float32 [1769472], P(('batch', 'seq')), may hold values from 0.2048 to 0.8192
- out_weight: float32 [589824], P(('batch', 'seq')), may hold values from -0.875 to 0.875
- out_first: float32 [589824], P(('batch', 'seq')), may hold values from -7 to 7
- out_second: float32 [589824], P(('batch', 'seq')), may hold values from 0.1024 to 0.4096
- up_weight: float32 [2359296], P(('batch', 'seq')), may hold values from -0.21875 to 0.21875
- up_first: float32 [2359296], P(('batch', 'seq')), may hold values from -10 to 10
- up_second: float32 [2359296], P(('batch', 'seq')), may hold values from 0.2048 to 0.8192
- down_weight: float32 [2359296], P(('batch', 'seq')), may hold values from -0.109375 to 0.109375
- down_first: float32 [2359296], P(('batch', 'seq')), may hold values from -16 to 16
- down_second: float32 [2359296], P(('batch', 'seq')), may hold values from 0.6144 to 2.4576
- vec_weight: float32 [9216], P(('batch', 'seq'))
- vec_first: float32 [9216], P(('batch', 'seq')), may hold values from -16 to 16
- vec_second: float32 [9216], P(('batch', 'seq')), may hold values from 0.6144 to 2.4576
Outputs:
- output: bfloat16 [64, 512, 768], P('batch', 'seq')
- in_grad: float32 [64, 512, 768], P('batch', 'seq')
- qkv_master: float32 [1769472], P(('batch', 'seq'))
- qkv_moment: float32 [1769472], P(('batch', 'seq'))
- qkv_square: float32 [1769472], P(('batch', 'seq'))
- qkv_copy: bfloat16 [1769472], P(('batch', 'seq'))
- out_master: float32 [589824], P(('batch', 'seq'))
- out_moment: float32 [589824], P(('batch', 'seq'))
- out_square: float32 [589824], P(('batch', 'seq'))
- out_copy: bfloat16 [589824], P(('batch', 'seq'))
- up_master: float32 [2359296], P(('batch', 'seq'))
- up_moment: float32 [2359296], P(('batch', 'seq'))
- up_square: float32 [2359296], P(('batch', 'seq'))
- up_copy: bfloat16 [2359296], P(('batch', 'seq'))
- down_master: float32 [2359296], P(('batch', 'seq'))
- down_moment: float32 [2359296], P(('batch', 'seq'))
- down_square: float32 [2359296], P(('batch', 'seq'))
- down_copy: bfloat16 [2359296], P(('batch', 'seq'))
- vec_master: float32 [9216], P(('batch', 'seq'))
- vec_moment: float32 [9216], P(('batch', 'seq'))
- vec_square: float32 [9216], P(('batch', 'seq'))
- vec_copy: bfloat16 [9216], P(('batch', 'seq'))
The draws below stay inside these ranges and needn't reach their ends.
Inputs may be any that keep to these rules, and one draw needn't show every extreme that they name: `lengths`: in every group of 8 consecutive sequences one has length 512 and another a quarter of 512. word_spans[s, i] = (start, count) with start + count <= lengths[s] and count at most 4; used slots come first, each sequence uses 1 to 31 slots; an unused slot is (0, 0). In every sequence of length 512 the first slot is (511, 1).
All inputs are finite; a program needn't handle non-finite values.
Results may differ from the reference program's by a relative error of at most 0.014.
The reference program's roundings to bfloat16 on the way count: a program that leaves them out, or rounds other values in their place, can miss the bound.
Values may be sent and summed in bfloat16 or wider, within the bound.
A program may use at most 192 MiB of HBM per device.

```python
import math
import jax
import jax.numpy as jnp
from jax import lax

D = 768
HEADS = 12
HDIM = 64
FF = 3072
LEN = 512
SEQ_DEV = 8
NSPAN = 32
STEP = 10
SEQS = 64
VEC = 9216


def length_table(key):
    group_count = SEQS // SEQ_DEV
    key_base, key_top, key_gap = jax.random.split(key, 3)
    base_length = jax.random.randint(key_base, (group_count, SEQ_DEV), LEN // 4, LEN + 1)
    longest = jax.random.randint(key_top, (group_count, 1), 0, SEQ_DEV)
    shortest = (longest + jax.random.randint(key_gap, (group_count, 1), 1, SEQ_DEV)) % SEQ_DEV
    column = jnp.arange(SEQ_DEV, dtype=jnp.int32)[None, :]
    picked = jnp.where(column == longest, LEN, jnp.where(column == shortest, LEN // 4, base_length))
    return picked.reshape(SEQS).astype(jnp.int32)


def draw_lengths(key, part):
    return length_table(key)


def draw_word_spans(key, part):
    seq_lengths = length_table(key)
    key = jax.random.fold_in(key, 5)
    key_level, key_jitter, key_start, key_size = jax.random.split(key, 4)
    group_count = SEQS // SEQ_DEV
    count_level = jax.random.randint(key_level, (group_count, 1), 1, NSPAN)
    jitter = jax.random.randint(key_jitter, (group_count, SEQ_DEV), -2, 3)
    counts = jnp.clip(count_level + jitter, 1, NSPAN - 1).reshape(SEQS, 1)
    starts = jax.random.randint(key_start, (SEQS, NSPAN), 0, seq_lengths[:, None])
    span_sizes = jax.random.randint(key_size, (SEQS, NSPAN), 1, 5)
    span_sizes = jnp.minimum(span_sizes, seq_lengths[:, None] - starts)
    slot_number = jnp.arange(NSPAN, dtype=jnp.int32)[None, :]
    forced = (seq_lengths[:, None] == LEN) & (slot_number == 0)
    starts = jnp.where(forced, LEN - 1, starts)
    span_sizes = jnp.where(forced, 1, span_sizes)
    in_use = slot_number < counts
    starts = jnp.where(in_use, starts, 0)
    span_sizes = jnp.where(in_use, span_sizes, 0)
    return jnp.stack([starts, span_sizes], axis=-1).astype(jnp.int32)


def draw_vec_weight(key, part):
    key = jax.random.fold_in(key, 9)
    key_gain, key_bias = jax.random.split(key, 2)
    position = jnp.arange(VEC, dtype=jnp.int32)
    is_gain = (position >= 3 * D) & (position < 4 * D) | (position >= 6 * D + FF) & (position < 7 * D + FF)
    gains = 1.0 + 0.3 * jax.random.uniform(key_gain, (VEC,), jnp.float32, -1.0, 1.0)
    biases = 0.3 * jax.random.normal(key_bias, (VEC,), jnp.float32)
    return jnp.where(is_gain, gains, biases).astype(jnp.float32)


def shard_levels(own_key, dims, cuts, least, largest):
    level, own = 1.0, jax.random.fold_in(own_key, 6)
    for axis_at, parts in cuts:
        draws = jnp.exp(jax.random.uniform(jax.random.fold_in(own, axis_at), (parts,), jnp.float32, least / len(cuts), largest / len(cuts)))
        level = level * jnp.repeat(draws, dims[axis_at] // parts).reshape([-1 if axis == axis_at else 1 for axis in range(len(dims))])
    return level


def gaussian(own_key, extent, width, most, cuts=(), kind=jnp.bfloat16):
    gain = shard_levels(own_key, extent, cuts, -0.22, 0.18) if cuts else 1.0
    values = jax.random.normal(own_key, extent, jnp.float32) * width * gain
    return jnp.minimum(jnp.maximum(values, -most), most).astype(kind)


def setup_inputs(seed: int = 0) -> dict:
    key_list = jax.random.split(jax.random.key(seed), 20)
    return {
        "inputs": gaussian(key_list[0], (SEQS, LEN, D), 1.0, 6.0, ((0, 8), (1, 4))),
        "out_grad": gaussian(key_list[1], (SEQS, LEN, D), 1.0, 6.0, ((0, 8), (1, 4))),
        "lengths": draw_lengths(jax.random.fold_in(key_list[19], 71), 0),
        "word_spans": draw_word_spans(jax.random.fold_in(key_list[19], 71), 0),
        "qkv_weight": gaussian(key_list[4], (3 * D * D,), D ** -0.5, 0.21875, ((0, 32),), jnp.float32),
        "qkv_first": gaussian(key_list[5], (3 * D * D,), (0.035 * (SEQS * NSPAN) ** 0.5), 10.0, ((0, 32),), jnp.float32),
        "qkv_second": jnp.clip(jnp.exp(math.log(0.8192) - 1.3862944 * jax.random.uniform(key_list[6], (3 * D * D,), jnp.float32) ** shard_levels(key_list[6], (3 * D * D,), ((0, 32),), -0.2, 0.2)), 0.2048, 0.8192),
        "out_weight": gaussian(key_list[7], (D * D,), (D // 16) ** -0.5, 0.875, ((0, 32),), jnp.float32),
        "out_first": gaussian(key_list[8], (D * D,), (0.024 * (SEQS * NSPAN) ** 0.5), 7.0, ((0, 32),), jnp.float32),
        "out_second": jnp.clip(jnp.exp(math.log(0.4096) - 1.3862944 * jax.random.uniform(key_list[9], (D * D,), jnp.float32) ** shard_levels(key_list[9], (D * D,), ((0, 32),), -0.2, 0.2)), 0.1024, 0.4096),
        "up_weight": gaussian(key_list[10], (D * FF,), D ** -0.5, 0.21875, ((0, 32),), jnp.float32),
        "up_first": gaussian(key_list[11], (D * FF,), (0.035 * (SEQS * NSPAN) ** 0.5), 10.0, ((0, 32),), jnp.float32),
        "up_second": jnp.clip(jnp.exp(math.log(0.8192) - 1.3862944 * jax.random.uniform(key_list[12], (D * FF,), jnp.float32) ** shard_levels(key_list[12], (D * FF,), ((0, 32),), -0.2, 0.2)), 0.2048, 0.8192),
        "down_weight": gaussian(key_list[13], (FF * D,), FF ** -0.5, 0.109375, ((0, 32),), jnp.float32),
        "down_first": gaussian(key_list[14], (FF * D,), (0.06 * (SEQS * NSPAN) ** 0.5), 16.0, ((0, 32),), jnp.float32),
        "down_second": jnp.clip(jnp.exp(math.log(2.4576) - 1.3862944 * jax.random.uniform(key_list[15], (FF * D,), jnp.float32) ** shard_levels(key_list[15], (FF * D,), ((0, 32),), -0.2, 0.2)), 0.6144, 2.4576),
        "vec_weight": draw_vec_weight(jax.random.fold_in(key_list[19], 71), 0),
        "vec_first": gaussian(key_list[17], (VEC,), (0.06 * (SEQS * NSPAN) ** 0.5), 16.0, ((0, 32),), jnp.float32),
        "vec_second": jnp.clip(jnp.exp(math.log(2.4576) - 1.3862944 * jax.random.uniform(key_list[18], (VEC,), jnp.float32) ** shard_levels(key_list[18], (VEC,), ((0, 32),), -0.2, 0.2)), 0.6144, 2.4576),
    }


EXACT_PRECISION = lax.Precision.HIGHEST
NORM_EPS = 1e-12
ADAM_EPS = 1e-08
FIRST_DECAY = 0.9
SECOND_DECAY = 0.999
NEG_LARGE = -1000000000.0

@jax.custom_vjp
def reduced_input(v):
    return lax.optimization_barrier(v.astype(jnp.bfloat16)).astype(jnp.float32)

@jax.custom_vjp
def reduced_backward(v):
    return v

def low_keep(v):
    return (reduced_input(v), None)

def low_pass(kept, grad):
    return (grad,)

def back_keep(v):
    return (v, None)

def back_low(kept, grad):
    return (reduced_input(grad),)
reduced_input.defvjp(low_keep, low_pass)
reduced_backward.defvjp(back_keep, back_low)

def layer_norm(residual, gain_vector, offset):
    center = residual - lax.optimization_barrier(jnp.mean(residual, axis=-1, keepdims=True))
    spread = lax.optimization_barrier(jnp.mean(center * center, axis=-1, keepdims=True))
    return center * lax.rsqrt(spread + NORM_EPS) * gain_vector + offset

def gelu_exact(values_in):
    return jax.nn.gelu(values_in, approximate=False)

def split_vector(vector):
    boundaries = [0, D, 2 * D, 3 * D, 4 * D, 5 * D, 5 * D + FF, 6 * D + FF, 7 * D + FF, 8 * D + FF]
    return [vector[boundaries[number]:boundaries[number + 1]] for number in range(9)]

def span_rows(word_spans, places):
    starts = word_spans[:, :, 0][:, :, None]
    counts = word_spans[:, :, 1][:, :, None]
    inside = (places[None, None, :] >= starts) & (places[None, None, :] < starts + counts)
    return jnp.any(inside, axis=1)

def layer_forward(inputs, lengths, query_key_value_weight, output_proj_weight, up_proj_weight, down_proj_weight, vector):
    seq_count = inputs.shape[0]
    seq_len = inputs.shape[1]
    bias_q, bias_v, output_proj_bias, gain_one, shift_one, up_proj_bias, down_proj_bias, gain_two, shift_two = split_vector(vector)
    head_scale = 1.0 / math.sqrt(HDIM)
    projected_output = jnp.einsum('crg,gt->crt', inputs, query_key_value_weight, precision=EXACT_PRECISION)
    queries = reduced_backward(reduced_input((projected_output[..., :D] + bias_q) * head_scale)).reshape(seq_count, seq_len, HEADS, HDIM)
    key_heads = reduced_backward(reduced_input(projected_output[..., D:2 * D])).reshape(seq_count, seq_len, HEADS, HDIM)
    value_heads = reduced_backward(reduced_input(projected_output[..., 2 * D:] + bias_v)).reshape(seq_count, seq_len, HEADS, HDIM)
    scores = reduced_backward(jnp.einsum('sqhd,skhd->shqk', queries, key_heads, precision=EXACT_PRECISION))
    places = jnp.arange(seq_len, dtype=jnp.int32)
    valid_keys = places[None, :] < lengths[:, None]
    scores = jnp.where(valid_keys[:, None, None, :], scores, NEG_LARGE)
    row_top = lax.optimization_barrier(jnp.max(scores, axis=-1, keepdims=True))
    exp_scores = jnp.exp(scores - row_top)
    prob_values = reduced_input(exp_scores / lax.optimization_barrier(jnp.sum(exp_scores, axis=-1, keepdims=True)))
    mixed = jnp.einsum('shqk,skhd->sqhd', prob_values, value_heads, precision=EXACT_PRECISION).reshape(seq_count, seq_len, D)
    attended_values = reduced_backward(reduced_input(mixed))
    residual_branch = reduced_backward(jnp.einsum('crg,gt->crt', attended_values, output_proj_weight, precision=EXACT_PRECISION) + output_proj_bias)
    attention_normed = layer_norm(inputs + residual_branch, gain_one, shift_one)
    inner_preactivation = reduced_backward(jnp.einsum('pvb,bc->pvc', reduced_input(attention_normed), up_proj_weight, precision=EXACT_PRECISION) + up_proj_bias)
    active_hidden = reduced_input(gelu_exact(inner_preactivation))
    second_normed = reduced_backward(jnp.einsum('axo,oq->axq', active_hidden, down_proj_weight, precision=EXACT_PRECISION) + down_proj_bias)
    result = layer_norm(attention_normed + second_normed, gain_two, shift_two)
    return result * valid_keys[:, :, None].astype(result.dtype)

def adam_update(master, first_moment, second_moment, gradient, step_rate, decay_rate):
    new_first = FIRST_DECAY * first_moment + (1.0 - FIRST_DECAY) * gradient
    new_second = SECOND_DECAY * second_moment + (1.0 - SECOND_DECAY) * gradient * gradient
    first_hat = new_first / (1.0 - FIRST_DECAY ** STEP)
    second_hat = new_second / (1.0 - SECOND_DECAY ** STEP)
    new_master = master - step_rate * (first_hat / (jnp.sqrt(second_hat) + ADAM_EPS) + decay_rate * master)
    return (new_master, new_first, new_second, new_master.astype(jnp.bfloat16))

def reference(inputs, out_grad, lengths, word_spans, qkv_weight, qkv_first, qkv_second, out_weight, out_first, out_second, up_weight, up_first, up_second, down_weight, down_first, down_second, vec_weight, vec_first, vec_second):
    masters = (qkv_weight, out_weight, up_weight, down_weight, vec_weight)
    shape_list = ((D, 3 * D), (D, D), (D, FF), (FF, D), (VEC,))
    lowered = [master.astype(jnp.bfloat16).astype(jnp.float32).reshape(shape_of) for master, shape_of in zip(masters, shape_list)]
    group_count = SEQS // SEQ_DEV
    grouped = (inputs.reshape(group_count, SEQ_DEV, LEN, D), out_grad.reshape(group_count, SEQ_DEV, LEN, D), lengths.reshape(group_count, SEQ_DEV), word_spans.reshape(group_count, SEQ_DEV, NSPAN, 2))
    places = jnp.arange(LEN, dtype=jnp.int32)

    def one_group(totals, packed):
        block_in, block_grad, block_lengths, block_spans = packed
        marked = span_rows(block_spans, places).astype(jnp.float32)
        cotangent = block_grad.astype(jnp.float32) * marked[:, :, None]

        def apply_layer(layer_input, query_key_value_weight, output_proj_weight, up_proj_weight, down_proj_weight, vector):
            return layer_forward(layer_input, block_lengths, query_key_value_weight, output_proj_weight, up_proj_weight, down_proj_weight, vector)
        result, pullback = jax.vjp(apply_layer, block_in.astype(jnp.float32), *lowered)
        grads = pullback(cotangent)
        totals = tuple((total + gradient for total, gradient in zip(totals, grads[1:])))
        return (totals, (result.astype(jnp.bfloat16), grads[0]))
    zero_sums = tuple((jnp.zeros(weight.shape, jnp.float32) for weight in lowered))
    totals, (outputs, in_grads) = lax.scan(one_group, zero_sums, grouped)
    output = outputs.reshape(SEQS, LEN, D)
    in_grad = in_grads.reshape(SEQS, LEN, D)
    matrix_rate = 1.6 / math.sqrt(D)
    qkv_new = adam_update(qkv_weight, qkv_first, qkv_second, totals[0].reshape(-1), matrix_rate, 0.01)
    out_new = adam_update(out_weight, out_first, out_second, totals[1].reshape(-1), matrix_rate, 0.01)
    up_new = adam_update(up_weight, up_first, up_second, totals[2].reshape(-1), matrix_rate, 0.01)
    down_new = adam_update(down_weight, down_first, down_second, totals[3].reshape(-1), 1.6 / math.sqrt(FF), 0.01)
    vec_new = adam_update(vec_weight, vec_first, vec_second, totals[4], 0.4, 0.0)
    return (output, in_grad, qkv_new[0], qkv_new[1], qkv_new[2], qkv_new[3], out_new[0], out_new[1], out_new[2], out_new[3], up_new[0], up_new[1], up_new[2], up_new[3], down_new[0], down_new[1], down_new[2], down_new[3], vec_new[0], vec_new[1], vec_new[2], vec_new[3])
```

```python
import math

import jax
import jax.numpy as jnp
from jax import lax
from jax.sharding import PartitionSpec as P
from jax.experimental import pallas as pl
from jax.experimental.pallas import tpu as pltpu

D = 768
HDIM = 64
FF = 3072
STEP = 10


NORM_EPS = 1e-12
ADAM_EPS = 1e-08
FIRST_DECAY = 0.9
SECOND_DECAY = 0.999
NEG_LARGE = -1000000000.0


MESH = pl.DeviceIdType.MESH

BF, F32 = jnp.bfloat16, jnp.float32

def al(v, n=128):
    return pl.multiple_of(v, n)

class Ctx:
    def __init__(self):
        self.b = lax.axis_index("batch"); self.s = lax.axis_index("seq")
        self.z = lax.div(self.b, 2); self.y = lax.rem(self.b, 2)
        self.x = lax.div(self.s, 2); self.c = lax.rem(self.s, 2)
        self.zp = [(lax.rem(self.z + j, 4) * 2 + self.y, self.s) for j in (1, 2, 3)]
        self.xp = (self.b, (1 - self.x) * 2 + self.c)
        self.yp = (self.z * 2 + 1 - self.y, self.s)
        self.sib = (self.b, self.x * 2 + 1 - self.c)
        self.sp = [(self.b, lax.rem(self.s + j, 4)) for j in (1, 2, 3)]

def barrier(cx):
    sem = pltpu.get_barrier_semaphore()
    peers = cx.zp + [cx.yp] + cx.sp
    for p in peers:
        pl.semaphore_signal(sem, inc=1, device_id=p, device_id_type=MESH)
    pl.semaphore_wait(sem, len(peers))

def rcopy(src, dst, ss, rs, dev):
    return pltpu.make_async_remote_copy(src_ref=src, dst_ref=dst, send_sem=ss, recv_sem=rs, device_id=dev, device_id_type=MESH)

def chunk_list():
    out = []
    for base in (D, 2 * D, 0):
        out.append(("q", base, D // 2))
    out.append(("o", 0, D // 2))
    for base in (0, FF // 2):
        out.append(("u", base, FF // 4))
    for base in (0, D // 2):
        out.append(("d", base, D // 2))
    return out

CH = chunk_list()
NC = len(CH)

def ag_kernel(inp, og, qf, of, uf, df, wq, wo, wu, wd, xs, os_,
              s24q, s24o, s24u, sib_q, sib_o, sib_u,
              ssem, rsem, fsem, gsem, tsem, rtsem, lsem):
    cx = Ctx()
    W = {"q": wq, "o": wo, "u": wu, "d": wd}
    barrier(cx)
    def tok(src, dst, base):
        cps = []
        me = cx.s
        for j in range(3):
            o = cx.sp[j][1]
            cps.append(rcopy(src.at[pl.ds(o * 2, 2)], dst.at[:, pl.ds(al(me * 128), 128)],
                             tsem.at[base + j], rtsem.at[base + j], cx.sp[j]))
        loc = pltpu.make_async_copy(src.at[pl.ds(me * 2, 2)], dst.at[:, pl.ds(al(me * 128), 128)], lsem.at[base // 3])
        for c in cps: c.start()
        loc.start()
        return cps + [loc]
    t_in = tok(inp, xs, 0)
    for ref, dst, C in ((qf, s24q, 3 * D), (of, s24o, D), (uf, s24u, FF)):
        n = C // 128
        for k in range(n):
            dst[:, 128 * k:128 * (k + 1)] = ref[pl.ds(k, 24, stride=n), :]
    fx = {}
    oc = 1 - cx.c
    for i, (w, base, h) in enumerate(CH):
        if w == "d": continue
        s24, sb = {"q": (s24q, sib_q), "o": (s24o, sib_o), "u": (s24u, sib_u)}[w]
        fx[i] = rcopy(s24.at[:, pl.ds(al(base + oc * h), h)], sb.at[:, pl.ds(base // 2, h)], fsem.at[i], gsem.at[i], cx.sib)
        fx[i].start()
    def cols(i, plane):
        w, base, h = CH[i]
        if w == "d":
            return slice(None), slice(None)
        return None
    def view(i, zi, yi, xi, plane):
        w, base, h = CH[i]
        if w == "d":
            return W[w].at[zi, yi, xi, pl.ds(al(plane * 96, 96), 96), pl.ds(base, h)]
        return W[w].at[zi, yi, xi, :, pl.ds(al(base + plane * h), h)]
    live = []
    def start(c):
        c.start(); live.append(c); return c
    for i, (w, base, h) in enumerate(CH):
        if w == "d":
            if base == 0:
                for k in range(6):
                    wd[cx.z, cx.y, cx.x, pl.ds(al(cx.c * 96, 96), 96), 128 * k:128 * (k + 1)] = df[pl.ds(k, 96, stride=6), :].astype(BF)
    zc = {}
    def zstart(i):
        w, base, h = CH[i]
        if w != "d":
            s24, sb = {"q": (s24q, sib_q), "o": (s24o, sib_o), "u": (s24u, sib_u)}[w]
            fx[i].wait()
            mine = s24[:, pl.ds(al(base + cx.c * h), h)]
            theirs = sb[:, pl.ds(base // 2, h)]
            first = cx.c == 0
            top = jnp.where(first, mine, theirs); bot = jnp.where(first, theirs, mine)
            W[w][cx.z, cx.y, cx.x, :, pl.ds(al(base + cx.c * h), h)] = jnp.concatenate([top, bot], axis=0).astype(BF)
        v = view(i, cx.z, cx.y, cx.x, cx.c)
        zc[i] = [start(rcopy(v, v, ssem.at[i, j], rsem.at[i, j], cx.zp[j])) for j in range(3)]
    AHEAD = 2
    for i in range(AHEAD): zstart(i)
    A = slice(None)
    t_out = None
    xc, yc, sc = {}, {}, {i: [] for i in range(NC)}
    for t in range(NC + 2):
        if t < NC:
            for c in zc[t]: c.wait_recv()
            if t + AHEAD < NC: zstart(t + AHEAD)
            v = view(t, A, cx.y, cx.x, cx.c)
            xc[t] = start(rcopy(v, v, ssem.at[t, 3], rsem.at[t, 3], cx.xp))
            sc[t].append(start(rcopy(v, v, ssem.at[t, 5], rsem.at[t, 5], cx.sib)))
        if t == 4:
            t_out = tok(og, os_, 3)
        if 0 <= t - 1 < NC:
            i = t - 1
            xc[i].wait_recv()
            v = view(i, A, cx.y, A, cx.c)
            yc[i] = start(rcopy(v, v, ssem.at[i, 4], rsem.at[i, 4], cx.yp))
            v = view(i, A, cx.y, 1 - cx.x, cx.c)
            sc[i].append(start(rcopy(v, v, ssem.at[i, 6], rsem.at[i, 6], cx.sib)))
        if 0 <= t - 2 < NC:
            i = t - 2
            yc[i].wait_recv()
            v = view(i, A, 1 - cx.y, A, cx.c)
            sc[i].append(start(rcopy(v, v, ssem.at[i, 7], rsem.at[i, 7], cx.sib)))
    for i in range(NC):
        for c in sc[i]: c.wait_recv()
    for c in t_in + t_out: c.wait()
    for c in live: c.wait_send()

def ag_call(inp, og, qf, of, uf, df):
    V = pl.BlockSpec(memory_space=pltpu.VMEM); H = pl.BlockSpec(memory_space=pl.ANY)
    outs = [jax.ShapeDtypeStruct((4, 2, 2, 48, 3 * D), BF), jax.ShapeDtypeStruct((4, 2, 2, 48, D), BF),
            jax.ShapeDtypeStruct((4, 2, 2, 48, FF), BF), jax.ShapeDtypeStruct((4, 2, 2, 192, D), BF),
            jax.ShapeDtypeStruct((2, 512, D), BF), jax.ShapeDtypeStruct((2, 512, D), BF)]
    return pl.pallas_call(
        ag_kernel, out_shape=outs, in_specs=[H, H, V, V, V, V], out_specs=[V] * 6,
        scratch_shapes=[pltpu.VMEM((24, 3 * D), F32), pltpu.VMEM((24, D), F32), pltpu.VMEM((24, FF), F32),
                        pltpu.VMEM((24, 3 * D // 2), F32), pltpu.VMEM((24, D // 2), F32), pltpu.VMEM((24, FF // 2), F32),
                        pltpu.SemaphoreType.DMA((NC, 8)), pltpu.SemaphoreType.DMA((NC, 8)),
                        pltpu.SemaphoreType.DMA((NC,)), pltpu.SemaphoreType.DMA((NC,)),
                        pltpu.SemaphoreType.DMA((6,)), pltpu.SemaphoreType.DMA((6,)), pltpu.SemaphoreType.DMA((2,))],
        compiler_params=pltpu.CompilerParams(collective_id=0, has_side_effects=True, vmem_limit_bytes=60 * 2**20),
        name="gather",
    )(inp, og, qf, of, uf, df)


def from_behind(block, axis, distance):
    devices = range(lax.axis_size(axis))
    route = [((i - distance) % len(devices), i) for i in devices]
    return lax.ppermute(block, axis, route)


def layer_norm(residual, gain_vector, offset):
    center = residual - jnp.mean(residual, axis=-1, keepdims=True)
    spread = jnp.mean(center * center, axis=-1, keepdims=True)
    return center * lax.rsqrt(spread + NORM_EPS) * gain_vector + offset


def gelu_exact(values_in):
    return jax.nn.gelu(values_in, approximate=False)


def split_vector(vector):
    boundaries = [0, D, 2 * D, 3 * D, 4 * D, 5 * D, 5 * D + FF, 6 * D + FF, 7 * D + FF, 8 * D + FF]
    return [vector[boundaries[number] : boundaries[number + 1]] for number in range(9)]


def span_rows(word_spans, places):
    starts = word_spans[:, :, 0][:, :, None]
    counts = word_spans[:, :, 1][:, :, None]
    inside = (places[None, None, :] >= starts) & (places[None, None, :] < starts + counts)
    return jnp.any(inside, axis=1)


def adam_update(master, first_moment, second_moment, gradient, step_rate, decay_rate):
    new_first = FIRST_DECAY * first_moment + (1.0 - FIRST_DECAY) * gradient
    new_second = SECOND_DECAY * second_moment + (1.0 - SECOND_DECAY) * gradient * gradient
    first_hat = new_first / (1.0 - FIRST_DECAY**STEP)
    second_hat = new_second / (1.0 - SECOND_DECAY**STEP)
    new_master = master - step_rate * (
        first_hat / (jnp.sqrt(second_hat) + ADAM_EPS) + decay_rate * master
    )
    return (new_master, new_first, new_second, new_master.astype(jnp.bfloat16))


def masked_scores(query_h, keys_h, key_mask):
    raw_scores = jnp.einsum("sqd,skd->sqk", query_h, keys_h, preferred_element_type=jnp.float32)
    return jnp.where(key_mask[:, None, :], raw_scores, NEG_LARGE)


def make_forward(key_mask):

    def head_forward(packed):
        query_h, keys_h, values_h = packed
        scores = masked_scores(query_h, keys_h, key_mask)
        row_top = jnp.max(scores, axis=-1, keepdims=True)
        exp_scores = jnp.exp(scores - row_top)
        row_total = jnp.sum(exp_scores, axis=-1, keepdims=True)
        weights = (exp_scores / row_total).astype(jnp.bfloat16)
        mixed = jnp.einsum("sqk,skd->sqd", weights, values_h, preferred_element_type=jnp.float32)
        return (mixed, row_top, row_total)

    return head_forward


def make_back(key_mask):

    def head_back(packed):
        query_h, keys_one, values_one, grad_h, mixed_one, row_top, row_total = packed
        scores = masked_scores(query_h, keys_one, key_mask)
        prob_values = jnp.exp(scores - row_top) / row_total
        grad_probs = jnp.einsum(
            "sqd,skd->sqk", grad_h, values_one, preferred_element_type=jnp.float32
        )
        row_delta = jnp.sum(grad_h.astype(jnp.float32) * mixed_one, axis=-1, keepdims=True)
        grad_scores = (prob_values * (grad_probs - row_delta)).astype(jnp.bfloat16)
        grad_query = jnp.einsum(
            "sqk,skd->sqd", grad_scores, keys_one, preferred_element_type=jnp.float32
        )
        grad_keys = jnp.einsum(
            "sqk,sqd->skd", grad_scores, query_h, preferred_element_type=jnp.float32
        )
        grad_values = jnp.einsum(
            "sqk,sqd->skd",
            prob_values.astype(jnp.bfloat16),
            grad_h,
            preferred_element_type=jnp.float32,
        )
        return (grad_query, grad_keys, grad_values)

    return head_back


def to_heads(flat_rows):
    return flat_rows.reshape(flat_rows.shape[0], flat_rows.shape[1], -1, HDIM).transpose(2, 0, 1, 3)


def from_heads(head_major):
    return head_major.transpose(1, 2, 0, 3).reshape(head_major.shape[1], head_major.shape[2], -1)


def on_device(
    inputs,
    out_grad,
    lengths,
    word_spans,
    qkv_weight,
    qkv_first,
    qkv_second,
    out_weight,
    out_first,
    out_second,
    up_weight,
    up_first,
    up_second,
    down_weight,
    down_first,
    down_second,
    vec_weight,
    vec_first,
    vec_second,
):
    if lax.axis_size("batch") == 8:
        parts = ag_call(inputs, out_grad, qkv_weight.reshape(-1, 128), out_weight.reshape(-1, 128),
                        up_weight.reshape(-1, 128), down_weight.reshape(-1, 128))[:4]
    else:
        parts = [lax.all_gather(w.astype(BF), ("batch", "seq"), axis=0, tiled=True)
                 for w in (qkv_weight, out_weight, up_weight, down_weight)]
    gathered = list(parts) + [lax.all_gather(vec_weight.astype(BF), ("batch", "seq"), axis=0, tiled=True)]
    query_key_value_weight = gathered[0].reshape(D, 3 * D)
    output_proj_weight = gathered[1].reshape(D, D)
    up_proj_weight = gathered[2].reshape(D, FF)
    down_proj_weight = gathered[3].reshape(FF, D)
    vector = gathered[4].astype(jnp.float32)
    (
        bias_q,
        bias_v,
        output_proj_bias,
        gain_one,
        shift_one,
        up_proj_bias,
        down_proj_bias,
        gain_two,
        shift_two,
    ) = split_vector(vector)
    seq_count, block_len, _ = inputs.shape
    row_count = seq_count * block_len
    cycle_size = lax.axis_size("seq")
    cycle_here = lax.axis_index("seq")
    offsets = jnp.arange(block_len, dtype=jnp.int32)
    places = cycle_here * block_len + offsets
    row_valid = (places[None, :] < lengths[:, None]).astype(jnp.float32).reshape(row_count, 1)
    marked = span_rows(word_spans, places).astype(jnp.float32).reshape(row_count, 1)
    flat_in = inputs.reshape(row_count, D)
    head_scale = 1.0 / math.sqrt(HDIM)
    projected_output = jnp.dot(flat_in, query_key_value_weight, preferred_element_type=jnp.float32)
    queries = ((projected_output[:, :D] + bias_q) * head_scale).astype(jnp.bfloat16)
    own_pair = jnp.stack(
        [projected_output[:, D : 2 * D], projected_output[:, 2 * D :] + bias_v]
    ).astype(jnp.bfloat16)
    kept_pairs = [own_pair]
    moving = own_pair
    for cycle_step in range(1, cycle_size):
        moving = from_behind(moving, "seq", 1)
        kept_pairs.append(moving)
    sources = [(cycle_here - cycle_step) % cycle_size for cycle_step in range(cycle_size)]
    key_places = jnp.concatenate([source * block_len + offsets for source in sources])
    key_valid = key_places[None, :] < lengths[:, None]
    key_rows = jnp.concatenate(
        [cycle_pair[0].reshape(seq_count, block_len, D) for cycle_pair in kept_pairs], axis=1
    )
    value_rows = jnp.concatenate(
        [cycle_pair[1].reshape(seq_count, block_len, D) for cycle_pair in kept_pairs], axis=1
    )
    keys_h = to_heads(key_rows)
    values_h = to_heads(value_rows)
    query_heads = to_heads(queries.reshape(seq_count, block_len, D))
    mixed_heads, row_tops, totals = lax.map(
        make_forward(key_valid), (query_heads, keys_h, values_h)
    )
    attended_values = from_heads(mixed_heads).reshape(row_count, D).astype(jnp.bfloat16)
    residual_branch = (
        jnp.dot(attended_values, output_proj_weight, preferred_element_type=jnp.float32)
        + output_proj_bias
    )
    attention_normed, pull_first = jax.vjp(
        layer_norm, flat_in.astype(jnp.float32) + residual_branch, gain_one, shift_one
    )
    first_low = attention_normed.astype(jnp.bfloat16)
    inner_preactivation = (
        jnp.dot(first_low, up_proj_weight, preferred_element_type=jnp.float32) + up_proj_bias
    )
    active_hidden, pull_active = jax.vjp(gelu_exact, inner_preactivation)
    active_low = active_hidden.astype(jnp.bfloat16)
    second_normed = (
        jnp.dot(active_low, down_proj_weight, preferred_element_type=jnp.float32) + down_proj_bias
    )
    normed, pull_second = jax.vjp(layer_norm, attention_normed + second_normed, gain_two, shift_two)
    output = (normed * row_valid).astype(jnp.bfloat16).reshape(seq_count, block_len, D)
    cotangent = out_grad.reshape(row_count, D).astype(jnp.float32) * marked * row_valid
    grad_two, grad_gain_two, grad_shift_two = pull_second(cotangent)
    grad_second = grad_two.astype(jnp.bfloat16)
    grad_bias_down = jnp.sum(grad_second.astype(jnp.float32), axis=0)
    grad_down = jnp.einsum("rf,rd->fd", active_low, grad_second, preferred_element_type=jnp.float32)
    grad_active = jnp.einsum(
        "rd,fd->rf", grad_second, down_proj_weight, preferred_element_type=jnp.float32
    )
    grad_inner = pull_active(grad_active)[0].astype(jnp.bfloat16)
    grad_bias_up = jnp.sum(grad_inner.astype(jnp.float32), axis=0)
    grad_up = jnp.einsum("rd,rf->df", first_low, grad_inner, preferred_element_type=jnp.float32)
    grad_first = grad_two + jnp.einsum(
        "rf,df->rd", grad_inner, up_proj_weight, preferred_element_type=jnp.float32
    )
    grad_one, grad_gain_one, grad_shift_one = pull_first(grad_first)
    grad_branch = grad_one.astype(jnp.bfloat16)
    grad_bias_o = jnp.sum(grad_branch.astype(jnp.float32), axis=0)
    grad_out = jnp.einsum(
        "rd,re->de", attended_values, grad_branch, preferred_element_type=jnp.float32
    )
    grad_attended = jnp.einsum(
        "re,de->rd", grad_branch, output_proj_weight, preferred_element_type=jnp.float32
    ).astype(jnp.bfloat16)
    grad_heads = to_heads(grad_attended.reshape(seq_count, block_len, D))
    query_grads, key_grads, value_grads = lax.map(
        make_back(key_valid),
        (query_heads, keys_h, values_h, grad_heads, mixed_heads, row_tops, totals),
    )
    pieces = [
        jnp.stack(
            [
                from_heads(
                    key_grads[:, :, cycle_step * block_len : (cycle_step + 1) * block_len]
                ).reshape(row_count, D),
                from_heads(
                    value_grads[:, :, cycle_step * block_len : (cycle_step + 1) * block_len]
                ).reshape(row_count, D),
            ]
        )
        for cycle_step in range(cycle_size)
    ]
    summed = pieces[cycle_size - 1]
    for cycle_step in range(cycle_size - 1, 0, -1):
        summed = (
            from_behind(summed.astype(jnp.bfloat16), "seq", -1).astype(summed.dtype)
            + pieces[cycle_step - 1]
        )
    grad_query_low = (
        from_heads(query_grads).reshape(row_count, D).astype(jnp.bfloat16).astype(jnp.float32)
        * head_scale
    ).astype(jnp.bfloat16)
    grad_pair = summed.astype(jnp.bfloat16)
    grad_key_low = grad_pair[0]
    grad_value_low = grad_pair[1]
    grad_proj = jnp.concatenate([grad_query_low, grad_key_low, grad_value_low], axis=1)
    grad_qkv = jnp.einsum("rd,re->de", flat_in, grad_proj, preferred_element_type=jnp.float32)
    in_grad = grad_one + jnp.einsum(
        "re,de->rd", grad_proj, query_key_value_weight, preferred_element_type=jnp.float32
    )
    grad_bias_q = jnp.sum(grad_query_low.astype(jnp.float32), axis=0)
    grad_bias_v = jnp.sum(grad_value_low.astype(jnp.float32), axis=0)
    grad_vector = jnp.concatenate(
        [
            grad_bias_q,
            grad_bias_v,
            grad_bias_o,
            grad_gain_one,
            grad_shift_one,
            grad_bias_up,
            grad_bias_down,
            grad_gain_two,
            grad_shift_two,
        ]
    )
    grad_sums = (
        lax.psum_scatter(grad_qkv.reshape(-1), ("batch", "seq"), scatter_dimension=0, tiled=True),
        lax.psum_scatter(grad_out.reshape(-1), ("batch", "seq"), scatter_dimension=0, tiled=True),
        lax.psum_scatter(grad_up.reshape(-1), ("batch", "seq"), scatter_dimension=0, tiled=True),
        lax.psum_scatter(grad_down.reshape(-1), ("batch", "seq"), scatter_dimension=0, tiled=True),
        lax.psum_scatter(grad_vector, ("batch", "seq"), scatter_dimension=0, tiled=True),
    )
    matrix_rate = 1.6 / math.sqrt(D)
    qkv_new = adam_update(qkv_weight, qkv_first, qkv_second, grad_sums[0], matrix_rate, 0.01)
    out_new = adam_update(out_weight, out_first, out_second, grad_sums[1], matrix_rate, 0.01)
    up_new = adam_update(up_weight, up_first, up_second, grad_sums[2], matrix_rate, 0.01)
    down_new = adam_update(
        down_weight, down_first, down_second, grad_sums[3], 1.6 / math.sqrt(FF), 0.01
    )
    vec_new = adam_update(vec_weight, vec_first, vec_second, grad_sums[4], 0.4, 0.0)
    return (
        output,
        in_grad.reshape(seq_count, block_len, D),
        qkv_new[0],
        qkv_new[1],
        qkv_new[2],
        qkv_new[3],
        out_new[0],
        out_new[1],
        out_new[2],
        out_new[3],
        up_new[0],
        up_new[1],
        up_new[2],
        up_new[3],
        down_new[0],
        down_new[1],
        down_new[2],
        down_new[3],
        vec_new[0],
        vec_new[1],
        vec_new[2],
        vec_new[3],
    )


def solution(mesh):
    in_specs = (
        P("batch", "seq", None),
        P("batch", "seq", None),
        P("batch"),
        P("batch", None, None),
        P(("batch", "seq")),
        P(("batch", "seq")),
        P(("batch", "seq")),
        P(("batch", "seq")),
        P(("batch", "seq")),
        P(("batch", "seq")),
        P(("batch", "seq")),
        P(("batch", "seq")),
        P(("batch", "seq")),
        P(("batch", "seq")),
        P(("batch", "seq")),
        P(("batch", "seq")),
        P(("batch", "seq")),
        P(("batch", "seq")),
        P(("batch", "seq")),
    )
    out_specs = (
        P("batch", "seq", None),
        P("batch", "seq", None),
        P(("batch", "seq")),
        P(("batch", "seq")),
        P(("batch", "seq")),
        P(("batch", "seq")),
        P(("batch", "seq")),
        P(("batch", "seq")),
        P(("batch", "seq")),
        P(("batch", "seq")),
        P(("batch", "seq")),
        P(("batch", "seq")),
        P(("batch", "seq")),
        P(("batch", "seq")),
        P(("batch", "seq")),
        P(("batch", "seq")),
        P(("batch", "seq")),
        P(("batch", "seq")),
        P(("batch", "seq")),
        P(("batch", "seq")),
        P(("batch", "seq")),
        P(("batch", "seq")),
    )
    return jax.shard_map(
        on_device, mesh=mesh, in_specs=in_specs, out_specs=out_specs, check_vma=False
    )
```

```python
import math

import jax
import jax.numpy as jnp
from jax import lax
from jax.experimental import pallas as pl
from jax.experimental.pallas import tpu as pltpu
from jax.sharding import PartitionSpec as P

D = 768
HDIM = 64
FF = 3072
STEP = 10
LEN = 512
BLK = 128
SLOTS = 128
NSEQ = 2
ROWS = NSEQ * LEN
MROWS = NSEQ * SLOTS
VEC = 9216
VROWS = 9

NORM_EPS = 1e-12
ADAM_EPS = 1e-08
FIRST_DECAY = 0.9
SECOND_DECAY = 0.999
NEG_LARGE = -1000000000.0

BF, F32 = jnp.bfloat16, jnp.float32
MESH = pl.DeviceIdType.MESH
ALL = slice(None)

BQ, BV, BO, G1, S1, BU, BD, G2, S2 = 0, 768, 1536, 2304, 3072, 3840, 6912, 7680, 8448

CHUNKS = [
    ("q", D, 384, "A"),
    ("q", 2 * D, 384, "A"),
    ("q", 0, 384, "A"),
    ("o", 0, 384, "A"),
    ("u", 0, 384, "A"),
    ("u", D, 384, "A"),
    ("u", 2 * D, 384, "A"),
    ("u", 3 * D, 384, "A"),
    ("d", 0, 256, "A"),
    ("d", 256, 256, "C"),
    ("d", 512, 256, "C"),
]
NCH = len(CHUNKS)
A_CHUNKS = [i for i in range(NCH) if CHUNKS[i][3] == "A"]
C_CHUNKS = [i for i in range(NCH) if CHUNKS[i][3] == "C"]
COLS = {"q": 3 * D, "o": D, "u": FF, "d": D}
PIECE = {"q": 48, "o": 48, "u": 48, "d": 192}
OWN_ROWS = {"q": 24, "o": 24, "u": 24, "d": 96}
NSEM = 230


def mult(value, step=128):
    return pl.multiple_of(value, step)


def dot(a, b):
    return lax.dot_general(a, b, (((1,), (0,)), ((), ())), preferred_element_type=F32)


def dot_nt(a, b):
    return lax.dot_general(a, b, (((1,), (1,)), ((), ())), preferred_element_type=F32)


def dot_tn(a, b):
    return lax.dot_general(a, b, (((0,), (0,)), ((), ())), preferred_element_type=F32)


def normalize(rows):
    center = rows - jnp.sum(rows, axis=-1, keepdims=True) * (1.0 / D)
    spread = jnp.sum(center * center, axis=-1, keepdims=True) * (1.0 / D)
    scale = lax.rsqrt(spread + NORM_EPS)
    return center * scale, scale


def norm_back(grad, gain, hat, scale):
    cg = grad * gain
    mean_one = jnp.sum(cg, axis=-1, keepdims=True) * (1.0 / D)
    mean_hat = jnp.sum(cg * hat, axis=-1, keepdims=True) * (1.0 / D)
    return scale * (cg - mean_one - hat * mean_hat)


def normal_cdf(v):
    return 0.5 * (1.0 + lax.erf(v * math.sqrt(0.5)))


def row_sum(rows):
    return jnp.sum(rows, axis=0, keepdims=True)


class Layer:
    def __init__(self, refs):
        self.__dict__.update(refs)
        self.b = lax.axis_index("batch")
        self.s = lax.axis_index("seq")


    def vec(self, first, count):
        return self.vrow[0:1, first : first + count]

    def vec_at(self, first, block, count):
        return self.vrow[0:1, pl.ds(mult(first + block * count), count)]

    def wcols(self, ref, first, count):
        return ref[:, :, :, :, pl.ds(first, count)].reshape(D, count)

    def load_vector(self):
        for r in range(VEC // 128):
            blk = r // VROWS
            line = self.vb[blk // 2, blk % 2, r % VROWS : r % VROWS + 1, :]
            self.vrow[0:1, 128 * r : 128 * r + 128] = line.astype(BF).astype(F32)

    def store_vector_grads(self):
        for r in range(VEC // 128):
            blk = r // VROWS
            self.gvb[blk // 2, blk % 2, r % VROWS : r % VROWS + 1, :] = self.gvrow[0:1, 128 * r : 128 * r + 128]


    def make_masks(self):
        place = lax.broadcasted_iota(jnp.int32, (8, LEN), 1)
        upper = (
            lax.broadcasted_iota(jnp.int32, (LEN, LEN), 0) < lax.broadcasted_iota(jnp.int32, (LEN, LEN), 1)
        ).astype(F32).astype(BF)
        slot = lax.broadcasted_iota(jnp.int32, (SLOTS, LEN), 0).astype(F32)
        for i in range(NSEQ):
            length = self.lengths[self.s * NSEQ + i]
            self.kbias[i] = jnp.where(place < length, 0.0, NEG_LARGE)
            starts = self.spans[self.s * NSEQ + i, :, 0:1]
            counts = self.spans[self.s * NSEQ + i, :, 1:2]
            spot = lax.broadcasted_iota(jnp.int32, (32, LEN), 1)
            inside = jnp.where((spot >= starts) & (spot < starts + counts), 1.0, 0.0)
            marked = jnp.max(inside, axis=0, keepdims=True)
            rank = dot(jnp.broadcast_to(marked, (16, LEN)).astype(BF), upper)[0:1]
            rank = jnp.where(marked > 0.5, rank, -1.0)
            self.sel[i] = jnp.where(slot == rank, 1.0, 0.0).astype(BF)


    def project(self, first, dst, bias, scale):
        def body(i, _):
            seq, blk = lax.div(i, 3), lax.rem(i, 3)
            acc = dot(self.xs[seq], self.wcols(self.wq, mult(first + blk * 256), 256))
            if bias is not None:
                acc = acc + self.vrow[0:1, pl.ds(mult(bias + blk * 256), 256)]
            if scale:
                acc = acc * (1.0 / math.sqrt(HDIM))
            dst[seq, :, pl.ds(mult(blk * 256), 256)] = acc.astype(BF)
            return 0

        lax.fori_loop(0, 3 * NSEQ, body, 0)

    def pick(self, src, dst):
        for i in range(NSEQ):
            dst[SLOTS * i : SLOTS * (i + 1)] = dot(self.sel[i], src[i]).astype(BF)

    def attend(self, lo, hi):
        low = lax.broadcasted_iota(jnp.int32, (256, 128), 1) < HDIM

        def body(i, _):
            seq, rest = lax.div(i, 12), lax.rem(i, 12)
            cols = pl.ds(mult(lax.div(rest, 2) * 128), 128)
            rows = pl.ds(mult(lax.rem(rest, 2) * 256, 256), 256)
            q = self.qs[seq, rows, cols].astype(F32)
            k = self.ks[seq, :, cols]
            v = self.vs[seq, :, cols]
            bias = self.kbias[seq, 0:1, :]
            outs = []
            for e in range(2):
                qe = jnp.where(low if e == 0 else jnp.logical_not(low), q, 0.0).astype(BF)
                scores = dot_nt(qe, k) + bias
                p = jnp.exp(scores - jnp.max(scores, axis=-1, keepdims=True))
                p = p * (1.0 / jnp.sum(p, axis=-1, keepdims=True))
                outs.append(dot(p.astype(BF), v))
            self.qs[seq, rows, cols] = jnp.where(low, outs[0], outs[1]).astype(BF)
            return 0

        lax.fori_loop(lo, hi, body, 0)

    def marked_branch(self):
        r = dot(self.am[...], self.wcols(self.wo, 0, D)) + self.vec(BO, D) + self.xm[...].astype(F32)
        hat, scale = normalize(r)
        self.f1[...] = hat
        self.sc1[...] = jnp.broadcast_to(scale, (MROWS, 128))
        first = hat * self.vec(G1, D) + self.vec(S1, D)
        self.f0[...] = first
        self.low[...] = first.astype(BF)

    def marked_up(self, fb):
        def body(j, _):
            cols = pl.ds(mult(fb * D + j * 256), 256)
            v = dot(self.low[...], self.wcols(self.wu, mult(fb * D + j * 256), 256))
            v = v + self.vrow[0:1, pl.ds(mult(BU + fb * D + j * 256), 256)]
            cdf = normal_cdf(v)
            self.act[:, cols] = (v * cdf).astype(BF)
            self.dgl[:, cols] = cdf + v * (jnp.exp(-0.5 * v * v) * (1.0 / math.sqrt(2.0 * math.pi)))
            return 0

        lax.fori_loop(0, 3, body, 0)

    def marked_down(self, first):
        w = self.wd[:, :, :, :, first : first + 256].reshape(FF, 256)
        self.f3[:, first : first + 256] = dot(self.act[...], w)

    def second_back(self):
        r = self.f0[...] + self.f3[...] + self.vec(BD, D)
        hat, scale = normalize(r)
        cot = self.cm[...].astype(F32)
        self.gvrow[0:1, S2 : S2 + D] = row_sum(cot)
        self.gvrow[0:1, G2 : G2 + D] = row_sum(cot * hat)
        g_two = norm_back(cot, self.vec(G2, D), hat, scale)
        self.f0[...] = g_two
        g_low = g_two.astype(BF)
        self.g2[...] = g_low
        self.gvrow[0:1, BD : BD + D] = row_sum(g_low.astype(F32))

    def grad_down(self, first):
        def body(i, _):
            zi, yi = lax.div(i, 2), lax.rem(i, 2)
            g = dot_tn(self.act[:, pl.ds(mult(i * 384), 384)], self.g2[:, first : first + 256])
            self.gd[zi, yi, :, :, first : first + 256] = g.astype(BF).reshape(2, 192, 256)
            return 0

        lax.fori_loop(0, 8, body, 0)

    def inner_back(self):
        def body(i, _):
            zi, yi = lax.div(i, 2), lax.rem(i, 2)
            cols = pl.ds(mult(i * 384), 384)
            g = dot_nt(self.g2[...], self.wd[zi, yi].reshape(384, D)) * self.dgl[:, cols]
            g = g.astype(BF)
            self.act[:, cols] = g
            self.gvrow[0:1, pl.ds(mult(BU + i * 384), 384)] = row_sum(g.astype(F32))
            return 0

        lax.fori_loop(0, 8, body, 0)

    def grad_up(self, fb):
        def body(j, _):
            first = mult(fb * D + j * 256)
            g = dot_tn(self.low[...], self.act[:, pl.ds(first, 256)])
            self.gu[:, :, :, :, pl.ds(first, 256)] = g.astype(BF).reshape(4, 2, 2, 48, 256)
            return 0

        lax.fori_loop(0, 3, body, 0)

    def first_back(self):
        def body(fb, _):
            w = self.wcols(self.wu, mult(fb * D), D)
            self.f0[...] += dot_nt(self.act[:, pl.ds(mult(fb * D), D)], w)
            return 0

        lax.fori_loop(0, 4, body, 0)
        grad = self.f0[...]
        hat = self.f1[...]
        self.gvrow[0:1, S1 : S1 + D] = row_sum(grad)
        self.gvrow[0:1, G1 : G1 + D] = row_sum(grad * hat)
        g_one = norm_back(grad, self.vec(G1, D), hat, self.sc1[:, 0:1])
        self.f0[...] = g_one
        g_low = g_one.astype(BF)
        self.g2[...] = g_low
        self.gvrow[0:1, BO : BO + D] = row_sum(g_low.astype(F32))
        self.ga[...] = dot_nt(g_low, self.wcols(self.wo, 0, D)).astype(BF)

    def grad_out(self):
        def body(j, _):
            cols = pl.ds(mult(j * 256), 256)
            g = dot_tn(self.am[...], self.g2[:, cols])
            self.go[:, :, :, :, cols] = g.astype(BF).reshape(4, 2, 2, 48, 256)
            return 0

        lax.fori_loop(0, 3, body, 0)

    def attend_back(self, lo, hi):
        low = lax.broadcasted_iota(jnp.int32, (SLOTS, 128), 1) < HDIM
        low_long = lax.broadcasted_iota(jnp.int32, (LEN, 128), 1) < HDIM

        def body(i, _):
            seq, hp = lax.div(i, 6), lax.rem(i, 6)
            cols = pl.ds(mult(hp * 128), 128)
            rows = pl.ds(mult(seq * SLOTS), SLOTS)
            q = self.qm[rows, cols]
            ga = self.ga[rows, cols]
            k = self.ks[seq, :, cols]
            v = self.vs[seq, :, cols]
            bias = self.kbias[seq, 0:1, :]
            gq, gk, gv = [], [], []
            for e in range(2):
                here = low if e == 0 else jnp.logical_not(low)
                qe = jnp.where(here, q.astype(F32), 0.0).astype(BF)
                gae = jnp.where(here, ga.astype(F32), 0.0).astype(BF)
                scores = dot_nt(qe, k) + bias
                p = jnp.exp(scores - jnp.max(scores, axis=-1, keepdims=True))
                p = p * (1.0 / jnp.sum(p, axis=-1, keepdims=True))
                dp = dot_nt(gae, v)
                gs = p * (dp - jnp.sum(p * dp, axis=-1, keepdims=True))
                gs = gs.astype(BF)
                gq.append(dot(gs, k))
                gk.append(dot_tn(gs, q))
                gv.append(dot_tn(p.astype(BF), ga))
            gql = jnp.where(low, gq[0], gq[1]).astype(BF).astype(F32) * (1.0 / math.sqrt(HDIM))
            self.gq[rows, cols] = gql.astype(BF)
            self.ks[seq, :, cols] = jnp.where(low_long, gk[0], gk[1]).astype(BF)
            self.vs[seq, :, cols] = jnp.where(low_long, gv[0], gv[1]).astype(BF)
            return 0

        lax.fori_loop(lo, hi, body, 0)

    def input_back(self):
        self.gvrow[0:1, BQ : BQ + D] = row_sum(self.gq[...].astype(F32))
        self.gvrow[0:1, BV : BV + D] = row_sum(self.vs[0].astype(F32)) + row_sum(self.vs[1].astype(F32))
        t = self.f0[...] + dot_nt(self.gq[...], self.wcols(self.wq, 0, D))
        hi = t.astype(BF)
        self.low[...] = hi
        self.g2[...] = (t - hi.astype(F32)).astype(BF)

        def body(i, _):
            seq, half = lax.div(i, 2), lax.rem(i, 2)
            rows = pl.ds(mult(half * 256, 256), 256)
            slots = pl.ds(mult(seq * SLOTS), SLOTS)
            acc = dot_nt(self.ks[seq, rows], self.wcols(self.wq, D, D))
            acc = acc + dot_nt(self.vs[seq, rows], self.wcols(self.wq, 2 * D, D))
            s = self.sel[seq, :, rows]
            acc = acc + (dot_tn(s, self.low[slots]) + dot_tn(s, self.g2[slots]))
            self.og[seq, rows] = acc.astype(BF)
            return 0

        lax.fori_loop(0, 4, body, 0)

    def grad_qkv(self, first):
        def body(j, _):
            cols = pl.ds(mult(j * 256), 256)
            if first == 0:
                g = dot_tn(self.xm[...], self.gq[:, cols])
            else:
                src = self.ks if first == D else self.vs
                g = dot_tn(self.xs[...].reshape(ROWS, D), src[:, :, cols].reshape(ROWS, 256))
            dst = pl.ds(mult(first + j * 256), 256)
            self.wq[:, :, :, :, dst] = g.astype(BF).reshape(4, 2, 2, 48, 256)
            return 0

        lax.fori_loop(0, 3, body, 0)

    def finish_rows(self, tile):
        seq, rows = tile // 2, slice(256 * (tile % 2), 256 * (tile % 2) + 256)
        r = dot(self.qs[seq, rows], self.wcols(self.wo, 0, D)) + self.vec(BO, D) + self.xs[seq, rows].astype(F32)
        hat, _ = normalize(r)
        first = hat * self.vec(G1, D) + self.vec(S1, D)
        self.tacc[...] = first + self.vec(BD, D)
        self.tlow[...] = first.astype(BF)

        def body(zi, _):
            v = dot(self.tlow[...], self.wcols(self.wu, mult(zi * D), D))
            v = v + self.vrow[0:1, pl.ds(mult(BU + zi * D), D)]
            a = (v * normal_cdf(v)).astype(BF)
            self.tacc[...] += dot(a, self.wd[zi].reshape(D, D))
            return 0

        lax.fori_loop(0, 4, body, 0)
        hat, _ = normalize(self.tacc[...])
        out = hat * self.vec(G2, D) + self.vec(S2, D)
        place = lax.broadcasted_iota(jnp.int32, (256, D), 0) + 256 * (tile % 2)
        out = jnp.where(place < self.lengths[self.s * NSEQ + seq], out, 0.0)
        self.qs[seq, rows] = out.astype(BF)


class Links(Layer):
    def __init__(self, refs):
        super().__init__(refs)
        b, s = self.b, self.s
        self.z, self.y = lax.div(b, 2), lax.rem(b, 2)
        self.x, self.c = lax.div(s, 2), lax.rem(s, 2)
        self.zpeers = [(lax.rem(self.z + j, 4) * 2 + self.y, s) for j in (1, 2, 3)]
        self.zfrom = [lax.rem(self.z + 4 - j, 4) for j in (1, 2, 3)]
        self.xpeer = (b, (1 - self.x) * 2 + self.c)
        self.ypeer = (self.z * 2 + 1 - self.y, s)
        self.twin = (b, self.x * 2 + 1 - self.c)
        self.speers = [(b, lax.rem(s + j, 4)) for j in (1, 2, 3)]
        self.used = 0
        self.live = []
        self.W = {"q": self.wq, "o": self.wo, "u": self.wu, "d": self.wd}
        self.G = {"q": self.wq, "o": self.go, "u": self.gu, "d": self.gd}

    def greet(self):
        sem = pltpu.get_barrier_semaphore()
        peers = self.zpeers + [self.ypeer] + self.speers
        for peer in peers:
            pl.semaphore_signal(sem, inc=1, device_id=peer, device_id_type=MESH)
        pl.semaphore_wait(sem, len(peers))

    def send(self, src, dst, peer):
        copy = pltpu.make_async_remote_copy(
            src_ref=src,
            dst_ref=dst,
            send_sem=self.ssem.at[self.used],
            recv_sem=self.rsem.at[self.used],
            device_id=peer,
            device_id_type=MESH,
        )
        self.used += 1
        copy.start()
        self.live.append(copy)
        return copy

    def local(self, src, dst, number):
        copy = pltpu.make_async_copy(src, dst, self.lsem.at[number])
        copy.start()
        return copy

    def release(self, mark):
        for copy in self.live[:mark]:
            copy.wait_send()
        self.live = self.live[mark:]

    def finish(self):
        self.release(len(self.live))


    def rows_in(self, src, dst, number):
        copies = []
        here = pl.ds(mult(self.s * BLK), BLK)
        for j in range(3):
            owner = self.speers[j][1]
            copies.append(self.send(src.at[pl.ds(owner * NSEQ, NSEQ)], dst.at[:, here], self.speers[j]))
        own = self.local(src.at[pl.ds(self.s * NSEQ, NSEQ)], dst.at[:, here], number)

        def wait():
            for copy in copies:
                copy.wait_recv()
            own.wait()

        return wait

    def rows_out(self, src, dst, seq, number):
        copies = []
        there = self.s * NSEQ + seq
        for j in range(3):
            owner = self.speers[j][1]
            copies.append(self.send(src.at[seq, pl.ds(mult(owner * BLK), BLK)], dst.at[there], self.speers[j]))
        own = self.local(src.at[seq, pl.ds(mult(self.s * BLK), BLK)], dst.at[there], number)

        def wait():
            for copy in copies:
                copy.wait_recv()
            own.wait()

        return wait


    def view(self, arrays, i, zi, yi, xi, plane):
        w, base, h, _ = CHUNKS[i]
        if w == "d":
            return arrays[w].at[zi, yi, xi, pl.ds(mult(plane * 96, 96), 96), pl.ds(base, h)]
        return arrays[w].at[zi, yi, xi, :, pl.ds(mult(base + plane * h), h)]

    def spot(self, i):
        w, base, h, _ = CHUNKS[i]
        return pl.ds(base if w == "d" else base // 2, h)


    def gather_start(self):
        self.greet()
        self.in_wait = self.rows_in(self.inp, self.xs, 0)
        vec_copies = [self.send(self.vec_in, self.v4.at[j], self.speers[j]) for j in range(3)]
        self.s24 = {"q": self.s24q, "o": self.s24o, "u": self.s24u}
        self.sib = {"q": self.sibq, "o": self.sibo, "u": self.sibu}
        flat = {"q": self.fq, "o": self.fo, "u": self.fu}
        self.fx = {}
        for w in ("q", "o", "u"):
            n = COLS[w] // 128
            for k in range(n):
                self.s24[w][:, 128 * k : 128 * (k + 1)] = flat[w][pl.ds(k, 24, stride=n), :]
            for i in A_CHUNKS:
                if CHUNKS[i][0] == w:
                    _, base, h, _ = CHUNKS[i]
                    src = self.s24[w].at[:, pl.ds(mult(base + (1 - self.c) * h), h)]
                    self.fx[i] = self.send(src, self.sib[w].at[:, self.spot(i)], self.twin)
            if w == "q":
                self.zc = {}
                self.gather_own(0)
        for k in range(6):
            rows = pl.ds(mult(self.c * 96, 96), 96)
            self.wd[self.z, self.y, self.x, rows, 128 * k : 128 * (k + 1)] = self.fd[pl.ds(k, 96, stride=6), :].astype(BF)
        self.cx = {}
        for i in C_CHUNKS:
            v = self.view(self.W, i, self.z, self.y, self.x, self.c)
            self.cx[i] = self.send(v, v, self.xpeer)
        self.gather_own(1)
        self.gather_own(2)
        for copy in vec_copies:
            copy.wait_recv()
        self.vb[self.z, self.y] = self.vec_in[...] + self.v4[0] + self.v4[1] + self.v4[2]
        v = self.vb.at[self.z, self.y]
        self.vz = [self.send(v, v, peer) for peer in self.zpeers]
        self.xc, self.yc, self.tc = {}, {}, {i: [] for i in range(NCH)}
        self.cy, self.cz = {}, {}
        self.tick_no = 0

    def gather_own(self, n):
        if n >= len(A_CHUNKS):
            return
        i = A_CHUNKS[n]
        w, base, h, _ = CHUNKS[i]
        if w != "d":
            self.fx[i].wait_recv()
            mine = self.s24[w][:, pl.ds(mult(base + self.c * h), h)]
            theirs = self.sib[w][:, self.spot(i)]
            first = self.c == 0
            top = jnp.where(first, mine, theirs)
            bottom = jnp.where(first, theirs, mine)
            cols = pl.ds(mult(base + self.c * h), h)
            self.W[w][self.z, self.y, self.x, :, cols] = jnp.concatenate([top, bottom], axis=0).astype(BF)
        v = self.view(self.W, i, self.z, self.y, self.x, self.c)
        self.zc[i] = [self.send(v, v, peer) for peer in self.zpeers]

    def mirror(self, i, zi, yi, xi):
        v = self.view(self.W, i, zi, yi, xi, self.c)
        self.tc[i].append(self.send(v, v, self.twin))

    def gather_tick(self):
        t = self.tick_no
        self.tick_no += 1
        n = len(A_CHUNKS)
        x, y, z, c = self.x, self.y, self.z, self.c
        if t < n:
            i = A_CHUNKS[t]
            for copy in self.zc[i]:
                copy.wait_recv()
            self.gather_own(t + 3)
            v = self.view(self.W, i, ALL, y, x, c)
            self.xc[i] = self.send(v, v, self.xpeer)
            self.mirror(i, ALL, y, x)
        if 0 <= t - 1 < n:
            i = A_CHUNKS[t - 1]
            self.xc[i].wait_recv()
            v = self.view(self.W, i, ALL, y, ALL, c)
            self.yc[i] = self.send(v, v, self.ypeer)
            self.mirror(i, ALL, y, 1 - x)
        if 0 <= t - 3 < n:
            i = A_CHUNKS[t - 3]
            self.yc[i].wait_recv()
            self.mirror(i, ALL, 1 - y, ALL)
        if t == 1:
            for copy in self.vz:
                copy.wait_recv()
            v = self.vb.at[:, y]
            self.vy = self.send(v, v, self.ypeer)
            for i in C_CHUNKS:
                self.cx[i].wait_recv()
                v = self.view(self.W, i, z, y, ALL, c)
                self.cy[i] = self.send(v, v, self.ypeer)
        if t == 3:
            self.vy.wait_recv()
            self.out_wait = self.rows_in(self.outg, self.og, 1)
        for number, i in enumerate(C_CHUNKS):
            if t == 2 + 3 * number:
                self.cy[i].wait_recv()
                v = self.view(self.W, i, z, ALL, ALL, c)
                self.cz[i] = [self.send(v, v, peer) for peer in self.zpeers]
                self.mirror(i, z, ALL, ALL)
            if t == 6 + 4 * number:
                for copy, zi in zip(self.cz[i], self.zfrom):
                    copy.wait_recv()
                    self.mirror(i, zi, ALL, ALL)

    def need(self, i):
        last = A_CHUNKS.index(i) + 3 if i in A_CHUNKS else 6 + 4 * C_CHUNKS.index(i)
        while self.tick_no <= last:
            self.gather_tick()
        for copy in self.tc[i]:
            copy.wait_recv()


    def sums_start(self):
        self.R0 = {"q": self.r0q, "o": self.r0o, "u": self.r0u, "d": self.r0d}
        self.R1 = {"q": self.r1q, "o": self.r1o, "u": self.r1u, "d": self.r1d}
        self.R2 = {"q": self.r2q, "o": self.r2o, "u": self.r2u, "d": self.r2d}
        self.R3 = {"q": self.r3q, "o": self.r3o, "u": self.r3u, "d": self.r3d}
        self.FIN = {"q": self.finq, "o": self.fino, "u": self.finu, "d": self.find}
        self.FR = {"q": self.frq, "o": self.fro, "u": self.fru}
        self.OUT = {"q": self.outq, "o": self.outo, "u": self.outu, "d": self.outd}
        self.tw, self.sy, self.sx, self.sz, self.sc = {}, {}, {}, {}, {}
        self.queue = []
        self.sum_no = 0

    def sums_push(self, i):
        v = self.view(self.G, i, ALL, ALL, ALL, 1 - self.c)
        dst = self.R0[CHUNKS[i][0]].at[:, :, :, :, self.spot(i)]
        self.tw[i] = self.send(v, dst, self.twin)
        if CHUNKS[i][3] == "A":
            self.queue.append(i)

    def add_twin(self, i):
        w = CHUNKS[i][0]
        self.tw[i].wait_recv()

        def body(zi, _):
            v = self.view(self.G, i, zi, ALL, ALL, self.c)
            v[...] = v[...] + self.R0[w][zi, :, :, :, self.spot(i)]
            return 0

        lax.fori_loop(0, 4, body, 0)

    def sum_twin(self, i):
        self.add_twin(i)
        v = self.view(self.G, i, ALL, 1 - self.y, ALL, self.c)
        self.sy[i] = self.send(v, self.R1[CHUNKS[i][0]].at[:, :, :, self.spot(i)], self.ypeer)

    def sum_y(self, i):
        w = CHUNKS[i][0]
        self.sy[i].wait_recv()

        def body(zi, _):
            v = self.view(self.G, i, zi, self.y, ALL, self.c)
            v[...] = v[...] + self.R1[w][zi, :, :, self.spot(i)]
            return 0

        lax.fori_loop(0, 4, body, 0)
        v = self.view(self.G, i, ALL, self.y, 1 - self.x, self.c)
        self.sx[i] = self.send(v, self.R2[w].at[:, :, self.spot(i)], self.xpeer)

    def sum_x(self, i):
        w = CHUNKS[i][0]
        self.sx[i].wait_recv()
        v = self.view(self.G, i, ALL, self.y, self.x, self.c)
        v[...] = v[...] + self.R2[w][:, :, self.spot(i)]
        self.sz[i] = []
        for j in range(3):
            v = self.view(self.G, i, self.zpeers_z(j), self.y, self.x, self.c)
            self.sz[i].append(self.send(v, self.R3[w].at[j, :, self.spot(i)], self.zpeers[j]))

    def zpeers_z(self, j):
        return lax.rem(self.z + j + 1, 4)

    def sum_z(self, i):
        w = CHUNKS[i][0]
        for copy in self.sz[i]:
            copy.wait_recv()
        total = self.view(self.G, i, self.z, self.y, self.x, self.c)[...].astype(F32)
        for j in range(3):
            total = total + self.R3[w][j, :, self.spot(i)].astype(F32)
        self.FIN[w][:, self.spot(i)] = total
        self.sum_halves(i)

    def sum_halves(self, i):
        w = CHUNKS[i][0]
        if w != "d":
            src = self.FIN[w].at[pl.ds(mult((1 - self.c) * 24, 8), 24), self.spot(i)]
            self.sc[i] = self.send(src, self.FR[w].at[:, self.spot(i)], self.twin)

    def sum_write(self, i):
        w, base, h, _ = CHUNKS[i]
        n = COLS[w] // 128
        if w == "d":
            for k in range(base // 128, (base + h) // 128):
                self.outd[pl.ds(k, 96, stride=n), :] = self.find[:, 128 * k : 128 * (k + 1)]
            return
        self.sc[i].wait_recv()
        for plane in range(2):
            for k in range(h // 128):
                lc = base // 2 + 128 * k
                own = self.FIN[w][pl.ds(mult(self.c * 24, 8), 24), lc : lc + 128]
                other = self.FR[w][:, lc : lc + 128]
                val = jnp.where(self.c == plane, own, other)
                self.OUT[w][pl.ds((base + plane * h) // 128 + k, 24, stride=n), :] = val

    def c_twin(self, i):
        self.add_twin(i)
        at = pl.ds(CHUNKS[i][1] - 256, 256)
        self.sz[i] = []
        for j in range(3):
            v = self.view(self.G, i, self.zpeers_z(j), ALL, ALL, self.c)
            self.sz[i].append(self.send(v, self.rz.at[j, :, :, :, at], self.zpeers[j]))

    def c_z(self, i):
        at = pl.ds(CHUNKS[i][1] - 256, 256)
        for copy in self.sz[i]:
            copy.wait_recv()
        v = self.view(self.G, i, self.z, ALL, ALL, self.c)
        total = v[...].astype(F32)
        for j in range(3):
            total = total + self.rz[j, :, :, :, at].astype(F32)
        v[...] = total.astype(BF)
        v = self.view(self.G, i, self.z, 1 - self.y, ALL, self.c)
        self.sy[i] = self.send(v, self.ry.at[:, :, at], self.ypeer)

    def c_y(self, i):
        at = pl.ds(CHUNKS[i][1] - 256, 256)
        self.sy[i].wait_recv()
        v = self.view(self.G, i, self.z, self.y, ALL, self.c)
        v[...] = v[...] + self.ry[:, :, at]
        v = self.view(self.G, i, self.z, self.y, 1 - self.x, self.c)
        self.sx[i] = self.send(v, self.rx.at[:, at], self.xpeer)

    def c_x(self, i):
        at = pl.ds(CHUNKS[i][1] - 256, 256)
        self.sx[i].wait_recv()
        v = self.view(self.G, i, self.z, self.y, self.x, self.c)
        self.find[:, self.spot(i)] = v[...].astype(F32) + self.rx[:, at].astype(F32)
        self.sum_write(i)

    def sums_tick(self):
        t = self.sum_no
        self.sum_no += 1
        n = len(A_CHUNKS)
        queue = self.queue
        if t < n:
            self.sum_twin(queue[t])
        if 0 <= t - 2 < n:
            self.sum_y(queue[t - 2])
        if 0 <= t - 3 < n:
            self.sum_x(queue[t - 3])
        if 0 <= t - 4 < n:
            self.sum_z(queue[t - 4])
        if 0 <= t - 5 < n:
            self.sum_write(queue[t - 5])
        for number, i in enumerate(C_CHUNKS):
            at = 5 + 2 * number
            if t == at:
                self.c_z(i)
            if t == at + 1:
                self.c_y(i)
            if t == at + 2:
                self.c_x(i)

    def vector_sums(self):
        v = self.gvb.at[:, 1 - self.y]
        first = self.send(v, self.gvy, self.ypeer)
        yield
        first.wait_recv()
        for zi in range(4):
            self.gvb[zi, self.y] = self.gvb[zi, self.y] + self.gvy[zi]
        second = [
            self.send(self.gvb.at[self.zpeers_z(j), self.y], self.gvz.at[j], self.zpeers[j]) for j in range(3)
        ]
        yield
        for copy in second:
            copy.wait_recv()
        self.gvs[...] = self.gvb[self.z, self.y] + self.gvz[0] + self.gvz[1] + self.gvz[2]
        third = [self.send(self.gvs, self.gv4.at[j], self.speers[j]) for j in range(3)]
        yield
        for copy in third:
            copy.wait_recv()
        self.outv[...] = self.gvs[...] + self.gv4[0] + self.gv4[1] + self.gv4[2]
        yield


def linked_kernel(*refs):
    k = Links(dict(zip(LINKED_NAMES, refs)))
    k.gather_start()
    k.make_masks()
    k.gather_tick()
    k.gather_tick()
    k.gather_tick()
    k.gather_tick()
    k.load_vector()
    k.in_wait()
    k.pick(k.xs, k.xm)
    k.need(0)
    k.project(D, k.ks, None, False)
    k.need(1)
    k.project(2 * D, k.vs, BV, False)
    k.need(2)
    k.project(0, k.qs, BQ, True)
    k.pick(k.qs, k.qm)
    for part in range(4):
        k.attend(6 * part, 6 * part + 6)
        k.gather_tick()
    k.pick(k.qs, k.am)
    k.need(3)
    k.marked_branch()
    for fb in range(4):
        k.need(4 + fb)
        k.marked_up(fb)
    k.out_wait()
    k.pick(k.og, k.cm)
    for i in (9, 10, 8):
        k.need(i)
        k.marked_down(CHUNKS[i][1])
    k.second_back()
    gathered = len(k.live)
    k.sums_start()
    for i in (9, 10, 8):
        k.grad_down(CHUNKS[i][1])
        k.sums_push(i)
    for i in C_CHUNKS:
        k.c_twin(i)
    k.inner_back()
    k.sums_tick()
    for fb in range(2):
        k.grad_up(fb)
        k.sums_push(4 + fb)
    k.sums_tick()
    for fb in range(2, 4):
        k.grad_up(fb)
        k.sums_push(4 + fb)
    k.first_back()
    k.grad_out()
    k.sums_push(3)
    k.sums_tick()
    for part in range(3):
        k.attend_back(4 * part, 4 * part + 4)
        if part == 1:
            k.sums_tick()
    k.input_back()
    k.store_vector_grads()
    waits = [k.rows_out(k.og, k.out_ig, seq, 2 + seq) for seq in range(NSEQ)]
    vector = k.vector_sums()
    next(vector)
    k.release(gathered)
    for i in range(3):
        k.grad_qkv(CHUNKS[i][1])
        k.sums_push(i)
    k.sums_tick()
    for tile in range(4):
        k.finish_rows(tile)
        k.sums_tick()
        if tile % 2 == 1:
            waits.append(k.rows_out(k.qs, k.out_rows, tile // 2, 4 + tile // 2))
        next(vector, None)
    while k.sum_no < len(A_CHUNKS) + 6:
        k.sums_tick()
        next(vector, None)
    for wait in waits:
        wait()
    k.finish()


def plain_kernel(*refs):
    k = Layer(dict(zip(PLAIN_NAMES, refs)))
    pairs = [(k.inp, k.xs), (k.outg, k.og), (k.inq, k.wq), (k.ino, k.wo), (k.inu, k.wu), (k.ind, k.wd)]
    copies = [pltpu.make_async_copy(src, dst, k.lsem.at[n]) for n, (src, dst) in enumerate(pairs)]
    for copy in copies:
        copy.start()
    for copy in copies:
        copy.wait()
    k.make_masks()
    k.load_vector()
    k.pick(k.xs, k.xm)
    k.project(D, k.ks, None, False)
    k.project(2 * D, k.vs, BV, False)
    k.project(0, k.qs, BQ, True)
    k.pick(k.qs, k.qm)
    k.attend(0, 24)
    k.pick(k.qs, k.am)
    k.marked_branch()
    for fb in range(4):
        k.marked_up(fb)
    k.pick(k.og, k.cm)
    for first in (0, 256, 512):
        k.marked_down(first)
    k.second_back()
    for first in (0, 256, 512):
        k.grad_down(first)
    k.inner_back()
    for fb in range(4):
        k.grad_up(fb)
    k.first_back()
    k.grad_out()
    k.attend_back(0, 12)
    k.input_back()
    k.store_vector_grads()
    for first in (D, 2 * D, 0):
        k.grad_qkv(first)
    for tile in range(4):
        k.finish_rows(tile)
    pairs = [(k.qs, k.out_rows), (k.og, k.out_ig), (k.wq, k.outq), (k.go, k.outo), (k.gu, k.outu), (k.gd, k.outd)]
    copies = [pltpu.make_async_copy(src, dst, k.lsem.at[n]) for n, (src, dst) in enumerate(pairs)]
    for copy in copies:
        copy.start()
    for copy in copies:
        copy.wait()
    k.outv[...] = k.gvb[...]


def wshape(w):
    return (4, 2, 2, PIECE[w], COLS[w])


COMMON_SCRATCH = [
    ("wq", wshape("q"), BF),
    ("wo", wshape("o"), BF),
    ("wu", wshape("u"), BF),
    ("wd", wshape("d"), BF),
    ("xs", (NSEQ, LEN, D), BF),
    ("og", (NSEQ, LEN, D), BF),
    ("qs", (NSEQ, LEN, D), BF),
    ("ks", (NSEQ, LEN, D), BF),
    ("vs", (NSEQ, LEN, D), BF),
    ("sel", (NSEQ, SLOTS, LEN), BF),
    ("kbias", (NSEQ, 8, LEN), F32),
    ("vrow", (1, VEC), F32),
    ("gvrow", (1, VEC), F32),
    ("gvb", (4, 2, 16, 128), F32),
    ("xm", (MROWS, D), BF),
    ("am", (MROWS, D), BF),
    ("qm", (MROWS, D), BF),
    ("cm", (MROWS, D), BF),
    ("low", (MROWS, D), BF),
    ("g2", (MROWS, D), BF),
    ("ga", (MROWS, D), BF),
    ("gq", (MROWS, D), BF),
    ("f0", (MROWS, D), F32),
    ("f1", (MROWS, D), F32),
    ("f3", (MROWS, D), F32),
    ("sc1", (MROWS, 128), F32),
    ("act", (MROWS, FF), BF),
    ("dgl", (MROWS, FF), F32),
    ("gd", wshape("d"), BF),
    ("gu", wshape("u"), BF),
    ("go", wshape("o"), BF),
    ("tlow", (256, D), BF),
    ("tacc", (256, D), F32),
]


def linked_scratch():
    out = list(COMMON_SCRATCH)
    out += [("vb", (4, 2, 16, 128), F32), ("v4", (3, 16, 128), F32)]
    for w in ("q", "o", "u"):
        out += [("s24" + w, (24, COLS[w]), F32), ("sib" + w, (24, COLS[w] // 2), F32)]
    for w in ("q", "o", "u", "d"):
        rows = 96 if w == "d" else 48
        half = D if w == "d" else COLS[w] // 2
        part = 256 if w == "d" else half
        out += [
            ("r0" + w, (4, 2, 2, rows, half), BF),
            ("r1" + w, (4, 2, rows, part), BF),
            ("r2" + w, (4, rows, part), BF),
            ("r3" + w, (3, rows, part), BF),
            ("fin" + w, (rows, half), F32),
        ]
        if w != "d":
            out.append(("fr" + w, (24, half), F32))
    out += [
        ("rz", (3, 2, 2, 96, 512), BF),
        ("ry", (2, 96, 512), BF),
        ("rx", (96, 512), BF),
        ("gvy", (4, 16, 128), F32),
        ("gvz", (3, 16, 128), F32),
        ("gvs", (16, 128), F32),
        ("gv4", (3, 16, 128), F32),
    ]
    return out


LINKED_SCRATCH = linked_scratch()
LINKED_INS = ["lengths", "spans", "inp", "outg", "fq", "fo", "fu", "fd", "vec_in"]
LINKED_OUTS = ["out_rows", "out_ig", "outq", "outo", "outu", "outd", "outv"]
LINKED_NAMES = LINKED_INS + LINKED_OUTS + [n for n, _, _ in LINKED_SCRATCH] + ["ssem", "rsem", "lsem"]
PLAIN_INS = ["lengths", "spans", "inp", "outg", "inq", "ino", "inu", "ind", "vb"]
PLAIN_NAMES = PLAIN_INS + LINKED_OUTS + [n for n, _, _ in COMMON_SCRATCH] + ["lsem"]

IN_VMEM = pl.BlockSpec(memory_space=pltpu.VMEM)
IN_SMEM = pl.BlockSpec(memory_space=pltpu.SMEM)
ANYWHERE = pl.BlockSpec(memory_space=pl.ANY)


def flat_shape(w):
    return (OWN_ROWS[w] * COLS[w] // 128, 128)


def linked_call(lengths, spans, inp, outg, flats, vec_in):
    outs = [jax.ShapeDtypeStruct((8, BLK, D), BF)] * 2
    outs += [jax.ShapeDtypeStruct(flat_shape(w), F32) for w in ("q", "o", "u", "d")]
    outs += [jax.ShapeDtypeStruct((16, 128), F32)]
    return pl.pallas_call(
        linked_kernel,
        out_shape=outs,
        in_specs=[IN_SMEM, IN_VMEM, ANYWHERE, ANYWHERE] + [IN_VMEM] * 5,
        out_specs=[ANYWHERE, ANYWHERE] + [IN_VMEM] * 5,
        scratch_shapes=[pltpu.VMEM(shape, dtype) for _, shape, dtype in LINKED_SCRATCH]
        + [pltpu.SemaphoreType.DMA((NSEM,)), pltpu.SemaphoreType.DMA((NSEM,)), pltpu.SemaphoreType.DMA((8,))],
        compiler_params=pltpu.CompilerParams(
            collective_id=0, has_side_effects=True, vmem_limit_bytes=64 * 2**20 - 2**16
        ),
        name="layer",
    )(lengths, spans, inp, outg, *flats, vec_in)


def plain_call(lengths, spans, inp, outg, weights, vb):
    outs = [jax.ShapeDtypeStruct((NSEQ, LEN, D), BF)] * 2
    outs += [jax.ShapeDtypeStruct(wshape(w), BF) for w in ("q", "o", "u", "d")]
    outs += [jax.ShapeDtypeStruct((4, 2, 16, 128), F32)]
    return pl.pallas_call(
        plain_kernel,
        out_shape=outs,
        in_specs=[IN_SMEM, IN_VMEM] + [ANYWHERE] * 6 + [IN_VMEM],
        out_specs=[ANYWHERE] * 6 + [IN_VMEM],
        scratch_shapes=[pltpu.VMEM(shape, dtype) for _, shape, dtype in COMMON_SCRATCH]
        + [pltpu.SemaphoreType.DMA((8,))],
        compiler_params=pltpu.CompilerParams(vmem_limit_bytes=60 * 2**20),
        name="layer",
    )(lengths, spans, inp, outg, *weights, vb)


def adam_update(master, first_moment, second_moment, gradient, step_rate, decay_rate):
    new_first = FIRST_DECAY * first_moment + (1.0 - FIRST_DECAY) * gradient
    new_second = SECOND_DECAY * second_moment + (1.0 - SECOND_DECAY) * gradient * gradient
    first_hat = new_first / (1.0 - FIRST_DECAY**STEP)
    second_hat = new_second / (1.0 - SECOND_DECAY**STEP)
    new_master = master - step_rate * (
        first_hat / (jnp.sqrt(second_hat) + ADAM_EPS) + decay_rate * master
    )
    return (new_master, new_first, new_second, new_master.astype(jnp.bfloat16))


RATES = (1.6 / math.sqrt(D), 1.6 / math.sqrt(D), 1.6 / math.sqrt(D), 1.6 / math.sqrt(FF))


def adam_kernel(*refs):
    for n in range(4):
        grad, master, first, second = (refs[4 * n + m][...] for m in range(4))
        for out, value in zip(refs[16 + 4 * n : 20 + 4 * n], adam_update(master, first, second, grad, RATES[n], 0.01)):
            out[...] = value


def adam_call(groups):
    steps = 3
    specs, outs, out_specs, flat = [], [], [], []
    for group in groups:
        rows = group[0].shape[0]
        spec = pl.BlockSpec((rows // steps, 128), lambda i: (i, 0))
        specs += [spec] * 4
        out_specs += [spec] * 4
        outs += [jax.ShapeDtypeStruct((rows, 128), F32)] * 3 + [jax.ShapeDtypeStruct((rows, 128), BF)]
        flat += list(group)
    new = pl.pallas_call(
        adam_kernel,
        out_shape=outs,
        grid=(steps,),
        in_specs=specs,
        out_specs=out_specs,
        compiler_params=pltpu.CompilerParams(vmem_limit_bytes=32 * 2**20),
        name="adam",
    )(*flat)
    return [tuple(a.reshape(-1) for a in new[4 * n : 4 * n + 4]) for n in range(4)]


def on_device(
    inputs,
    out_grad,
    lengths,
    word_spans,
    qkv_weight,
    qkv_first,
    qkv_second,
    out_weight,
    out_first,
    out_second,
    up_weight,
    up_first,
    up_second,
    down_weight,
    down_first,
    down_second,
    vec_weight,
    vec_first,
    vec_second,
):
    groups = [
        (qkv_weight, qkv_first, qkv_second),
        (out_weight, out_first, out_second),
        (up_weight, up_first, up_second),
        (down_weight, down_first, down_second),
    ]
    everywhere = ("batch", "seq")
    if lax.axis_size("batch") == 8 and lax.axis_size("seq") == 4:
        place = lax.axis_index("seq")
        share = vec_weight.shape[0]
        vec_in = lax.dynamic_update_slice(jnp.zeros((16 * 128,), F32), vec_weight, (share * place,)).reshape(16, 128)
        flats = [group[0].reshape(-1, 128) for group in groups]
        rows, in_grad, *sums, vec_sum = linked_call(lengths, word_spans, inputs, out_grad, flats, vec_in)
        vec_grad = lax.dynamic_slice(vec_sum.reshape(-1), (share * place,), (share,))
        news = adam_call([(g,) + tuple(a.reshape(-1, 128) for a in group) for g, group in zip(sums, groups)])
        in_grad = in_grad.astype(F32)
    else:
        weights = [
            lax.all_gather(group[0].astype(BF), everywhere, axis=0, tiled=True).reshape(wshape(w))
            for w, group in zip("qoud", groups)
        ]
        vector = lax.all_gather(vec_weight.astype(BF), everywhere, axis=0, tiled=True).astype(F32)
        vb = jnp.pad(vector.reshape(4, 2, VROWS, 128), ((0, 0), (0, 0), (0, 16 - VROWS), (0, 0)))
        own = lax.axis_index("seq") * NSEQ
        xs, og = (
            lax.all_to_all(a, "seq", split_axis=0, concat_axis=1, tiled=True) for a in (inputs, out_grad)
        )
        rows, in_grad, *grads, gvb = plain_call(lengths, word_spans, xs, og, weights, vb)
        rows, in_grad = (
            lax.all_to_all(a, "seq", split_axis=1, concat_axis=0, tiled=True) for a in (rows, in_grad)
        )
        in_grad = in_grad.astype(F32)
        sums = [
            lax.psum_scatter(g.astype(F32).reshape(-1), everywhere, scatter_dimension=0, tiled=True) for g in grads
        ]
        vec_grad = lax.psum_scatter(
            gvb[:, :, :VROWS].reshape(-1), everywhere, scatter_dimension=0, tiled=True
        )
        news = [
            adam_update(master, first, second, g, rate, 0.01)
            for (master, first, second), g, rate in zip(groups, sums, RATES)
        ]
    vec_new = adam_update(vec_weight, vec_first, vec_second, vec_grad, 0.4, 0.0)
    flat = [array for new in news for array in new]
    return (rows, in_grad, *flat, *vec_new)


def solution(mesh):
    owned = P(("batch", "seq"))
    rows = P("batch", "seq", None)
    in_specs = (rows, rows, P("batch"), P("batch", None, None)) + (owned,) * 15
    out_specs = (rows, rows) + (owned,) * 20
    return jax.shard_map(on_device, mesh=mesh, in_specs=in_specs, out_specs=out_specs, check_vma=False)
```

```python
import math

import jax
import jax.numpy as jnp
from jax import lax
from jax.experimental import pallas as pl
from jax.experimental.pallas import tpu as pltpu
from jax.sharding import PartitionSpec as P

D = 768
HDIM = 64
FF = 3072
STEP = 10
LEN = 512
BLK = 128
SLOTS = 128
NSEQ = 2
ROWS = NSEQ * LEN
MROWS = NSEQ * SLOTS
VEC = 9216
VROWS = 9

NORM_EPS = 1e-12
ADAM_EPS = 1e-08
FIRST_DECAY = 0.9
SECOND_DECAY = 0.999
NEG_LARGE = -1000000000.0

BF, F32 = jnp.bfloat16, jnp.float32
MESH = pl.DeviceIdType.MESH
ALL = slice(None)

BQ, BV, BO, G1, S1, BU, BD, G2, S2 = 0, 768, 1536, 2304, 3072, 3840, 6912, 7680, 8448

K = "K"
V = "V"
Q = "Q"
O = "o"
U0 = "u0"
U1 = "u1"
U2 = "u2"
U3 = "u3"
D0 = "d0"
D1 = "d1"
D2 = "d2"
CHUNKS = {
    K: ("q", 768, 384, "zyx", "yxz"),
    V: ("q", 1536, 384, "zxy", "yxz"),
    Q: ("q", 0, 384, "zxy", "zyx"),
    O: ("o", 0, 384, "zxy", "yzx"),
    U0: ("u", 0, 384, "yzx", "xyz"),
    U1: ("u", 768, 384, "zyx", "xyz"),
    U2: ("u", 1536, 384, "yxz", "yxz"),
    U3: ("u", 2304, 384, "zyx", "yxz"),
    D0: ("d", 0, 256, "zxy", "xzy"),
    D1: ("d", 256, 256, "xzy", "zyx"),
    D2: ("d", 512, 256, "xzy", "yxz"),
}
COLS = {"q": 3 * D, "o": D, "u": FF, "d": D}
PIECE = {"q": 48, "o": 48, "u": 48, "d": 192}
OWN_ROWS = {"q": 24, "o": 24, "u": 24, "d": 96}
FULL = {"z": 4, "y": 2, "x": 2}
ATT_PARTS = 6
NSEND = 60
NRECV = 120


def mult(value, step=128):
    return pl.multiple_of(value, step)


def dot(a, b):
    return lax.dot_general(a, b, (((1,), (0,)), ((), ())), preferred_element_type=F32)


def dot_nt(a, b):
    return lax.dot_general(a, b, (((1,), (1,)), ((), ())), preferred_element_type=F32)


def dot_tn(a, b):
    return lax.dot_general(a, b, (((0,), (0,)), ((), ())), preferred_element_type=F32)


def normalize(rows):
    center = rows - jnp.sum(rows, axis=-1, keepdims=True) * (1.0 / D)
    spread = jnp.sum(center * center, axis=-1, keepdims=True) * (1.0 / D)
    scale = lax.rsqrt(spread + NORM_EPS)
    return center * scale, scale


def norm_back(grad, gain, hat, scale):
    cg = grad * gain
    mean_one = jnp.sum(cg, axis=-1, keepdims=True) * (1.0 / D)
    mean_hat = jnp.sum(cg * hat, axis=-1, keepdims=True) * (1.0 / D)
    return scale * (cg - mean_one - hat * mean_hat)


def normal_cdf(v):
    return 0.5 * (1.0 + lax.erf(v * math.sqrt(0.5)))


def row_sum(rows):
    return jnp.sum(rows, axis=0, keepdims=True)


class Layer:
    def __init__(self, refs):
        self.__dict__.update(refs)
        self.b = lax.axis_index("batch")
        self.s = lax.axis_index("seq")


    def vec(self, first, count):
        return self.vrow[0:1, first : first + count]

    def vec_at(self, first, block, count):
        return self.vrow[0:1, pl.ds(mult(first + block * count), count)]

    def wcols(self, ref, first, count):
        return ref[:, :, :, :, pl.ds(first, count)].reshape(D, count)

    def load_vector(self):
        for r in range(VEC // 128):
            blk = r // VROWS
            line = self.vb[blk // 2, blk % 2, r % VROWS : r % VROWS + 1, :]
            self.vrow[0:1, 128 * r : 128 * r + 128] = line.astype(BF).astype(F32)

    def store_vector_grads(self):
        for r in range(VEC // 128):
            blk = r // VROWS
            self.gvb[blk // 2, blk % 2, r % VROWS : r % VROWS + 1, :] = self.gvrow[0:1, 128 * r : 128 * r + 128]


    def make_masks(self):
        below = lax.broadcasted_iota(jnp.int32, (LEN, 128), 0)
        upper = (
            lax.broadcasted_iota(jnp.int32, (LEN, LEN), 0) < lax.broadcasted_iota(jnp.int32, (LEN, LEN), 1)
        ).astype(F32).astype(BF)
        slot = lax.broadcasted_iota(jnp.int32, (SLOTS, LEN), 0).astype(F32)
        for i in range(NSEQ):
            length = self.lengths[self.s * NSEQ + i]
            self.kmask[i] = jnp.where(below < length, 0.0, NEG_LARGE)
        for i, number in enumerate(self.mask_rows()):
            starts = self.spans[number, :, 0:1]
            counts = self.spans[number, :, 1:2]
            spot = lax.broadcasted_iota(jnp.int32, (32, LEN), 1)
            inside = jnp.where((spot >= starts) & (spot < starts + counts), 1.0, 0.0)
            marked = jnp.max(inside, axis=0, keepdims=True)
            rank = dot(jnp.broadcast_to(marked, (16, LEN)).astype(BF), upper)[0:1]
            rank = jnp.where(marked > 0.5, rank, -1.0)
            self.sel[i] = jnp.where(slot == rank, 1.0, 0.0).astype(BF)

    def mask_rows(self):
        return [self.s * NSEQ + i for i in range(NSEQ)]


    def project(self, first, dst, bias, scale):
        def body(i, _):
            seq, blk = lax.div(i, 3), lax.rem(i, 3)
            acc = dot(self.xs[seq], self.wcols(self.wq, mult(first + blk * 256), 256))
            if bias is not None:
                acc = acc + self.vrow[0:1, pl.ds(mult(bias + blk * 256), 256)]
            if scale:
                acc = acc * (1.0 / math.sqrt(HDIM))
            dst[seq, :, pl.ds(mult(blk * 256), 256)] = acc.astype(BF)
            return 0

        lax.fori_loop(0, 3 * NSEQ, body, 0)

    def pick(self, src, dst):
        for i in range(NSEQ):
            dst[SLOTS * i : SLOTS * (i + 1)] = dot(self.sel[i], src[i]).astype(BF)

    def head_keys(self, seq, cols):
        k = self.ks[seq, :, cols].astype(F32)
        lane = lax.broadcasted_iota(jnp.int32, (LEN, 128), 1)
        mask = self.kmask[seq]
        low = jnp.where(lane < HDIM, k, jnp.where(lane == HDIM, mask, 0.0)).astype(BF)
        high = jnp.where(lane >= HDIM, k, jnp.where(lane == 0, mask, 0.0)).astype(BF)
        return low, high

    def head_rows(self, rows, mark):
        r = rows.astype(F32)
        lane = lax.broadcasted_iota(jnp.int32, r.shape, 1)
        one = 1.0 if mark else 0.0
        low = jnp.where(lane < HDIM, r, jnp.where(lane == HDIM, one, 0.0)).astype(BF)
        high = jnp.where(lane >= HDIM, r, jnp.where(lane == 0, one, 0.0)).astype(BF)
        return low, high

    def attend(self, lo, hi):
        low = lax.broadcasted_iota(jnp.int32, (256, 128), 1) < HDIM

        def body(i, _):
            seq = lax.div(i, 6)
            cols = pl.ds(mult(lax.rem(i, 6) * 128), 128)
            keys = self.head_keys(seq, cols)
            v = jnp.concatenate([self.vs[seq, :, cols], jnp.ones((LEN, 128), BF)], axis=1)
            for rt in range(2):
                rows = slice(256 * rt, 256 * rt + 256)
                outs = []
                for qe, k in zip(self.head_rows(self.qs[seq, rows, cols], True), keys):
                    scores = dot_nt(qe, k)
                    p = jnp.exp(scores - jnp.max(scores, axis=-1, keepdims=True))
                    mixed = dot(p.astype(BF), v)
                    outs.append(mixed[:, :128] * (1.0 / mixed[:, 128:]))
                self.qs[seq, rows, cols] = jnp.where(low, outs[0], outs[1]).astype(BF)
            return 0

        lax.fori_loop(lo, hi, body, 0)

    def marked_branch(self):
        r = dot(self.am[...], self.wcols(self.wo, 0, D)) + self.vec(BO, D) + self.xm[...].astype(F32)
        hat, scale = normalize(r)
        self.f1[...] = hat
        self.sc1[...] = jnp.broadcast_to(scale, (MROWS, 128))
        first = hat * self.vec(G1, D) + self.vec(S1, D)
        self.f0[...] = first
        self.low[...] = first.astype(BF)

    def marked_up(self, fb):
        def body(j, _):
            cols = pl.ds(mult(fb * D + j * 256), 256)
            v = dot(self.low[...], self.wcols(self.wu, mult(fb * D + j * 256), 256))
            v = v + self.vrow[0:1, pl.ds(mult(BU + fb * D + j * 256), 256)]
            cdf = normal_cdf(v)
            self.act[:, cols] = (v * cdf).astype(BF)
            self.dgl[:, cols] = cdf + v * (jnp.exp(-0.5 * v * v) * (1.0 / math.sqrt(2.0 * math.pi)))
            return 0

        lax.fori_loop(0, 3, body, 0)

    def marked_down(self, first, count):
        w = self.wd[:, :, :, :, first : first + count].reshape(FF, count)
        self.f3[:, first : first + count] = dot(self.act[...], w)

    def second_back(self):
        r = self.f0[...] + self.f3[...] + self.vec(BD, D)
        hat, scale = normalize(r)
        cot = self.cm[...].astype(F32)
        self.gvrow[0:1, S2 : S2 + D] = row_sum(cot)
        self.gvrow[0:1, G2 : G2 + D] = row_sum(cot * hat)
        g_two = norm_back(cot, self.vec(G2, D), hat, scale)
        self.f0[...] = g_two
        g_low = g_two.astype(BF)
        self.g2[...] = g_low
        self.gvrow[0:1, BD : BD + D] = row_sum(g_low.astype(F32))

    def grad_down(self):
        def body(i, _):
            zi, yi = lax.div(i, 2), lax.rem(i, 2)
            g = dot_tn(self.act[:, pl.ds(mult(i * 384), 384)], self.g2[...])
            self.gd[zi, yi] = g.astype(BF).reshape(2, 192, D)
            return 0

        lax.fori_loop(0, 8, body, 0)

    def inner_back(self):
        def body(i, _):
            zi, yi = lax.div(i, 2), lax.rem(i, 2)
            cols = pl.ds(mult(i * 384), 384)
            g = dot_nt(self.g2[...], self.wd[zi, yi].reshape(384, D)) * self.dgl[:, cols]
            g = g.astype(BF)
            self.act[:, cols] = g
            self.gvrow[0:1, pl.ds(mult(BU + i * 384), 384)] = row_sum(g.astype(F32))
            return 0

        lax.fori_loop(0, 8, body, 0)

    def outer(self, left, right, dst, first):
        def body(m, _):
            g = dot_tn(left[:, pl.ds(mult(m * 384), 384)], right)
            dst[pl.ds(m * 2, 2), :, :, :, first : first + D] = g.astype(BF).reshape(2, 2, 2, 48, D)
            return 0

        lax.fori_loop(0, 2, body, 0)

    def grad_up(self, fb):
        self.outer(self.low, self.act[:, fb * D : fb * D + D], self.gu, fb * D)

    def first_back(self):
        def body(fb, _):
            w = self.wcols(self.wu, mult(fb * D), D)
            self.f0[...] += dot_nt(self.act[:, pl.ds(mult(fb * D), D)], w)
            return 0

        lax.fori_loop(0, 4, body, 0)
        grad = self.f0[...]
        hat = self.f1[...]
        self.gvrow[0:1, S1 : S1 + D] = row_sum(grad)
        self.gvrow[0:1, G1 : G1 + D] = row_sum(grad * hat)
        g_one = norm_back(grad, self.vec(G1, D), hat, self.sc1[:, 0:1])
        self.f0[...] = g_one
        g_low = g_one.astype(BF)
        self.g2[...] = g_low
        self.gvrow[0:1, BO : BO + D] = row_sum(g_low.astype(F32))
        self.ga[...] = dot_nt(g_low, self.wcols(self.wo, 0, D)).astype(BF)

    def grad_out(self):
        self.outer(self.am, self.g2[...], self.go, 0)

    def attend_back(self, lo, hi):
        low = lax.broadcasted_iota(jnp.int32, (SLOTS, 128), 1) < HDIM

        def body(i, _):
            seq, hp = lax.div(i, 6), lax.rem(i, 6)
            cols = pl.ds(mult(hp * 128), 128)
            rows = pl.ds(mult(seq * SLOTS), SLOTS)
            q = self.qm[rows, cols]
            ga = self.ga[rows, cols]
            v = self.vs[seq, :, cols]
            keys = self.head_keys(seq, cols)
            marks = self.head_rows(q, True)
            plain = self.head_rows(q, False)
            gas = self.head_rows(ga, False)
            gq, gss, ps = [], [], []
            for e in range(2):
                scores = dot_nt(marks[e], keys[e])
                p = jnp.exp(scores - jnp.max(scores, axis=-1, keepdims=True))
                p = p * (1.0 / jnp.sum(p, axis=-1, keepdims=True))
                dp = dot_nt(gas[e], v)
                gs = p * (dp - jnp.sum(p * dp, axis=-1, keepdims=True))
                gs = gs.astype(BF)
                gq.append(dot(gs, keys[e]))
                gss.append(gs)
                ps.append(p.astype(BF))
            gk = dot_tn(jnp.concatenate(gss, axis=0), jnp.concatenate(plain, axis=0))
            gv = dot_tn(jnp.concatenate(ps, axis=0), jnp.concatenate(gas, axis=0))
            gql = jnp.where(low, gq[0], gq[1]).astype(BF).astype(F32) * (1.0 / math.sqrt(HDIM))
            self.gq[rows, cols] = gql.astype(BF)
            self.ks[seq, :, cols] = gk.astype(BF)
            self.vs[seq, :, cols] = gv.astype(BF)
            return 0

        lax.fori_loop(lo, hi, body, 0)

    def input_back(self):
        self.gvrow[0:1, BQ : BQ + D] = row_sum(self.gq[...].astype(F32))
        self.gvrow[0:1, BV : BV + D] = row_sum(self.vs[0].astype(F32)) + row_sum(self.vs[1].astype(F32))
        t = self.f0[...] + dot_nt(self.gq[...], self.wcols(self.wq, 0, D))
        hi = t.astype(BF)
        self.ga[...] = hi
        self.cm[...] = (t - hi.astype(F32)).astype(BF)

        def body(i, _):
            seq, half = lax.div(i, 2), lax.rem(i, 2)
            rows = pl.ds(mult(half * 256, 256), 256)
            slots = pl.ds(mult(seq * SLOTS), SLOTS)
            acc = dot_nt(self.ks[seq, rows], self.wcols(self.wq, D, D))
            acc = acc + dot_nt(self.vs[seq, rows], self.wcols(self.wq, 2 * D, D))
            s = self.sel[seq, :, rows]
            acc = acc + (dot_tn(s, self.ga[slots]) + dot_tn(s, self.cm[slots]))
            self.og[half, seq] = acc.astype(BF)
            return 0

        lax.fori_loop(0, 4, body, 0)

    def grad_qkv(self, first):
        if first == 0:
            self.outer(self.xm, self.gq[...], self.wq, 0)
            return
        src = self.ks if first == D else self.vs

        def body(m, _):
            cols = pl.ds(mult(m * 384), 384)
            g = dot_tn(self.xs[:, :, cols].reshape(ROWS, 384), src[...].reshape(ROWS, D))
            self.wq[pl.ds(m * 2, 2), :, :, :, first : first + D] = g.astype(BF).reshape(2, 2, 2, 48, D)
            return 0

        lax.fori_loop(0, 2, body, 0)

    def finish_rows(self, tile):
        seq, rows = tile // 2, slice(256 * (tile % 2), 256 * (tile % 2) + 256)
        r = dot(self.qs[seq, rows], self.wcols(self.wo, 0, D)) + self.vec(BO, D) + self.xs[seq, rows].astype(F32)
        hat, _ = normalize(r)
        first = hat * self.vec(G1, D) + self.vec(S1, D)
        self.tacc[...] = first + self.vec(BD, D)
        self.tlow[...] = first.astype(BF)

        low = self.tlow[...]
        half = FF // 8

        def up(j):
            first = j * half
            return dot(low, self.wcols(self.wu, first, half)) + self.vec(BU + first, half)

        acc, v = self.tacc[...], up(0)
        for j in range(8):
            a = (v * normal_cdf(v)).astype(BF)
            if j < 7:
                v = up(j + 1)
            acc = acc + dot(a, self.wd[j // 2, j % 2].reshape(half, D))
        self.tacc[...] = acc
        hat, _ = normalize(self.tacc[...])
        out = hat * self.vec(G2, D) + self.vec(S2, D)
        place = lax.broadcasted_iota(jnp.int32, (256, D), 0) + 256 * (tile % 2)
        out = jnp.where(place < self.lengths[self.s * NSEQ + seq], out, 0.0)
        self.qs[seq, rows] = out.astype(BF)


class Links(Layer):
    def __init__(self, refs):
        super().__init__(refs)
        b, s = self.b, self.s
        self.z, self.y = lax.div(b, 2), lax.rem(b, 2)
        self.x, self.c = lax.div(s, 2), lax.rem(s, 2)
        self.zpeers = [(lax.rem(self.z + j, 4) * 2 + self.y, s) for j in (1, 2, 3)]
        self.zfrom = [lax.rem(self.z + 4 - j, 4) for j in (1, 2, 3)]
        self.xpeer = (b, (1 - self.x) * 2 + self.c)
        self.ypeer = (self.z * 2 + 1 - self.y, s)
        self.twin = (b, self.x * 2 + 1 - self.c)
        self.speers = [(b, lax.rem(s + j, 4)) for j in (1, 2, 3)]
        self.send_ids, self.recv_ids = {}, {}
        self.released = False
        self.W = {"q": self.wq, "o": self.wo, "u": self.wu, "d": self.wd}
        self.G = {"q": self.wq, "o": self.go, "u": self.gu, "d": self.gd}

    def greet(self):
        sem = pltpu.get_barrier_semaphore()
        peers = self.zpeers + [self.ypeer] + self.speers
        for peer in peers:
            pl.semaphore_signal(sem, inc=1, device_id=peer, device_id_type=MESH)
        pl.semaphore_wait(sem, len(peers))

    def send(self, src, dst, peer, recv, sent):
        ours = self.send_ids.setdefault(sent, len(self.send_ids))
        theirs = self.recv_ids.setdefault(recv, len(self.recv_ids))
        assert ours < NSEND and theirs < NRECV
        pltpu.make_async_remote_copy(
            src_ref=src,
            dst_ref=dst,
            send_sem=self.ssem.at[ours],
            recv_sem=self.rsem.at[theirs],
            device_id=peer,
            device_id_type=MESH,
        ).start()

    def arrived(self, recv, alike):
        pltpu.make_async_copy(alike, alike, self.rsem.at[self.recv_ids[recv]]).wait()

    def left(self, sent, alike):
        pltpu.make_async_copy(alike, alike, self.ssem.at[self.send_ids[sent]]).wait()

    def fifteen(self, name):
        return self.wu.at[0:4, 0:1, 0:1, :, 0:1920] if CHUNKS[name][0] == "d" else self.wu.at[0:3, 0:1, 0:1, :, 0 : 5 * CHUNKS[name][2]]

    def local(self, src, dst, number):
        copy = pltpu.make_async_copy(src, dst, self.lsem.at[number])
        copy.start()
        return copy

    def release_gather(self):
        for name in CHUNKS:
            self.left("g" + name, self.fifteen(name))
            self.left("m" + name, self.view(self.W, name, ALL, ALL, ALL, self.c))

    def finish(self):
        for name in CHUNKS:
            self.left("t" + name, self.__dict__["rt" + name])
            self.left("s" + name, self.fifteen(name))
        self.left("f", self.s24u)
        self.left("h", self.s24u)
        self.left("in", self.xs.at[:, 0:384])
        self.left("cot", self.og.at[0])
        self.left("far", self.cmx)
        for key in ("v4", "vz", "gz", "g4"):
            self.left(key, self.v4)
        for key in ("vy", "gy"):
            self.left(key, self.gvy)
        self.left("ig", self.out_ig.at[0:6])
        for seq in range(NSEQ):
            self.left("out%d" % seq, self.out_rows.at[0:3])


    def rows_in(self, src, dst):
        here = pl.ds(mult(self.s * BLK), BLK)
        for peer in self.speers:
            self.send(src.at[pl.ds(peer[1] * NSEQ, NSEQ)], dst.at[:, here], peer, "in", "in")
        self.in_own = self.local(src.at[pl.ds(self.s * NSEQ, NSEQ)], dst.at[:, here], 0)

    def rows_out(self, pick, dst, seq, key, number):
        there = self.s * NSEQ + seq
        for peer in self.speers:
            self.send(pick(peer[1]), dst.at[there], peer, key, key)
        self.waits.append(self.local(pick(self.s), dst.at[there], number))

    def do_igout(self):
        for seq in range(NSEQ):
            pick = lambda o, seq=seq: self.og.at[lax.div(o, 2), seq, pl.ds(mult(lax.rem(o, 2) * BLK), BLK)]
            self.rows_out(pick, self.out_ig, seq, "ig", 2 + seq)

    def do_out(self, seq):
        pick = lambda o: self.qs.at[seq, pl.ds(mult(o * BLK), BLK)]
        self.rows_out(pick, self.out_rows, seq, "out%d" % seq, 4 + seq)


    def mask_rows(self):
        other = self.xpeer[1]
        return [self.s * NSEQ + i for i in range(NSEQ)] + [other * NSEQ + i for i in range(NSEQ)]

    def cot_start(self):
        here = pl.ds(mult(self.c * BLK), BLK)
        twin = self.twin[1]
        other = lambda s: lax.rem(s + 2, 4)
        self.cot_own = []
        for half in range(2):
            mine = self.s if half == 0 else other(self.s)
            theirs = twin if half == 0 else other(twin)
            dst = self.og.at[half, :, here]
            self.cot_own.append(self.local(self.outg.at[pl.ds(mine * NSEQ, NSEQ)], dst, 6 + half))
            self.send(self.outg.at[pl.ds(theirs * NSEQ, NSEQ)], dst, self.twin, "cot", "cot")

    def do_tog(self):
        for copy in self.cot_own:
            copy.wait()
        self.arrived("cot", self.og.at[0])
        here = pl.ds(mult(self.x * 256, 256), 256)
        for i in range(NSEQ):
            rows = slice(SLOTS * i, SLOTS * (i + 1))
            self.cmx[rows] = dot(self.sel[NSEQ + i, :, here], self.og[1, i]).astype(BF)
        self.send(self.cmx, self.cmr, self.xpeer, "far", "far")

    def do_pickC(self):
        self.arrived("far", self.cmr)
        here = pl.ds(mult(self.x * 256, 256), 256)
        for i in range(NSEQ):
            rows = slice(SLOTS * i, SLOTS * (i + 1))
            near = dot(self.sel[i, :, here], self.og[0, i]).astype(BF)
            self.cm[rows] = near + self.cmr[rows]


    def view(self, arrays, name, zi, yi, xi, plane):
        w, base, h = CHUNKS[name][:3]
        if w == "d":
            return arrays[w].at[zi, yi, xi, pl.ds(mult(plane * 96, 96), 96), pl.ds(base, h)]
        return arrays[w].at[zi, yi, xi, :, pl.ds(mult(base + plane * h), h)]

    def boxed(self, arrays, name, box):
        return self.view(arrays, name, box["z"], box["y"], box["x"], self.c)

    def own_box(self):
        return {"z": pl.ds(self.z, 1), "y": pl.ds(self.y, 1), "x": pl.ds(self.x, 1)}

    def across(self, axis):
        if axis == "x":
            return [(pl.ds(1 - self.x, 1), self.xpeer)]
        if axis == "y":
            return [(pl.ds(1 - self.y, 1), self.ypeer)]
        return [(pl.ds(lax.rem(self.z + j + 1, 4), 1), self.zpeers[j]) for j in range(3)]

    def spot(self, name):
        w, base, h = CHUNKS[name][:3]
        return pl.ds(base if w == "d" else base // 2, h)


    def do_start(self):
        self.greet()
        self.waits = []
        self.rows_in(self.inp, self.xs)
        for j in range(3):
            self.send(self.vec_in, self.v4.at[j], self.speers[j], "v4", "v4")
        self.s24 = {"q": self.s24q, "o": self.s24o, "u": self.s24u}
        self.sib = {"q": self.sibq, "o": self.sibo, "u": self.sibu}
        flat = {"q": self.fq, "o": self.fo, "u": self.fu}
        self.have = set()
        for w in ("q", "o", "u"):
            n = COLS[w] // 128
            for k in range(n):
                self.s24[w][:, 128 * k : 128 * (k + 1)] = flat[w][pl.ds(k, 24, stride=n), :]
            for name, (cw, base, h, _, _) in CHUNKS.items():
                if cw == w:
                    src = self.s24[w].at[:, pl.ds(mult(base + (1 - self.c) * h), h)]
                    self.send(src, self.sib[w].at[:, self.spot(name)], self.twin, "f" + name, "f")
        for k in range(6):
            rows = pl.ds(mult(self.c * 96, 96), 96)
            self.wd[self.z, self.y, self.x, rows, 128 * k : 128 * (k + 1)] = self.fd[pl.ds(k, 96, stride=6), :].astype(BF)
        self.cot_start()
        self.sums_start()

    def own_piece(self, name):
        w, base, h = CHUNKS[name][:3]
        if w == "d":
            return
        self.arrived("f" + name, self.sib[w].at[:, self.spot(name)])
        mine = self.s24[w][:, pl.ds(mult(base + self.c * h), h)]
        theirs = self.sib[w][:, self.spot(name)]
        first = self.c == 0
        top = jnp.where(first, mine, theirs)
        bottom = jnp.where(first, theirs, mine)
        cols = pl.ds(mult(base + self.c * h), h)
        self.W[w][self.z, self.y, self.x, :, cols] = jnp.concatenate([top, bottom], axis=0).astype(BF)

    def mirror(self, name, box):
        v = self.boxed(self.W, name, box)
        self.send(v, v, self.twin, "m" + name, "m" + name)

    def do_ag(self, name, stage):
        order = CHUNKS[name][3]
        box = self.own_box()
        for axis in order[: max(stage - 1, 0)]:
            box[axis] = ALL
        if stage == 0:
            self.own_piece(name)
        else:
            axis = order[stage - 1]
            count = pl.ds(0, 3 if axis == "z" else 1)
            self.arrived((name, stage - 1), self.boxed(self.W, name, dict(box, **{axis: count})))
            if stage == 1:
                self.mirror(name, dict(box, **{axis: ALL}))
            elif axis == "z":
                for j in range(3):
                    self.mirror(name, dict(box, z=pl.ds(self.zfrom[j], 1)))
            else:
                self.mirror(name, dict(box, **{axis: self.across(axis)[0][0]}))
            box[axis] = ALL
        if stage < 3:
            v = self.boxed(self.W, name, box)
            for _, peer in self.across(order[stage]):
                self.send(v, v, peer, (name, stage), "g" + name)

    def need(self, *names):
        for name in names:
            if name not in self.have:
                self.have.add(name)
                self.arrived("m" + name, self.view(self.W, name, ALL, ALL, ALL, 1 - self.c))

    def need_weight(self, w, base=None):
        self.need(*[n for n, c in CHUNKS.items() if c[0] == w and (base is None or c[1] // D == base // D)])

    def do_vec0(self):
        self.arrived("v4", self.v4)
        self.vb[self.z, self.y] = self.vec_in[...] + self.v4[0] + self.v4[1] + self.v4[2]
        v = self.vb.at[self.z, self.y]
        for peer in self.zpeers:
            self.send(v, v, peer, "vz", "vz")

    def do_vec1(self):
        self.arrived("vz", self.v4)
        v = self.vb.at[:, self.y]
        self.send(v, v, self.ypeer, "vy", "vy")

    def do_vec(self):
        self.arrived("vy", self.gvy)
        self.load_vector()


    def sums_start(self):
        self.FIN = {"q": self.finq, "o": self.fino, "u": self.finu, "d": self.find}
        self.FR = {"q": self.frq, "o": self.fro, "u": self.fru}
        self.OUT = {"q": self.outq, "o": self.outo, "u": self.outu, "d": self.outd}

    def do_rs(self, name, stage):
        order = CHUNKS[name][4]
        if stage < 0:
            v = self.view(self.G, name, ALL, ALL, ALL, 1 - self.c)
            self.send(v, self.__dict__["rt" + name], self.twin, "t" + name, "t" + name)
            return
        if stage == 0:
            self.arrived("t" + name, self.__dict__["rt" + name])
        elif stage < 4:
            self.arrived(("s", name, stage - 1), self.__dict__["r%d" % (stage - 1) + name])
        elif CHUNKS[name][0] != "d":
            self.arrived("h" + name, self.FR[CHUNKS[name][0]].at[:, self.spot(name)])
        if stage == 4:
            self.sum_write(name)
            return
        box = {"z": ALL, "y": ALL, "x": ALL}
        own = self.own_box()
        for axis in order[:stage]:
            box[axis] = own[axis]
        if stage == 3:
            self.sum_last(name, box)
            return
        if stage == 0:
            self.add_parts(name, box, self.__dict__["rt" + name], False)
        else:
            self.add_parts(name, box, self.__dict__["r%d" % (stage - 1) + name], order[stage - 1] == "z")
        into = self.__dict__["r%d" % stage + name]
        for j, (index, peer) in enumerate(self.across(order[stage])):
            v = self.boxed(self.G, name, dict(box, **{order[stage]: index}))
            dst = into.at[pl.ds(j, 1)] if order[stage] == "z" else into
            self.send(v, dst, peer, ("s", name, stage), "s" + name)

    def add_parts(self, name, box, part, three):
        if three:
            v = self.boxed(self.G, name, box)
            total = v[...].astype(F32) + part[0:1].astype(F32)
            total = total + part[1:2].astype(F32) + part[2:3].astype(F32)
            v[...] = total.astype(BF)
        elif box["z"] is ALL:

            def body(zi, _):
                v = self.boxed(self.G, name, dict(box, z=pl.ds(zi, 1)))
                v[...] = v[...] + part[pl.ds(zi, 1)]
                return 0

            lax.fori_loop(0, 4, body, 0)
        else:
            v = self.boxed(self.G, name, box)
            v[...] = v[...] + part[...]

    def sum_last(self, name, box):
        w = CHUNKS[name][0]
        rows = 96 if w == "d" else 48
        part = self.__dict__["r2" + name]
        total = self.boxed(self.G, name, box)[...].astype(F32).reshape(rows, -1)
        for j in range(part.shape[0]):
            total = total + part[j, 0, 0].astype(F32)
        self.FIN[w][:, self.spot(name)] = total
        if w != "d":
            src = self.FIN[w].at[pl.ds(mult((1 - self.c) * 24, 8), 24), self.spot(name)]
            self.send(src, self.FR[w].at[:, self.spot(name)], self.twin, "h" + name, "h")

    def sum_write(self, name):
        w, base, h = CHUNKS[name][:3]
        n = COLS[w] // 128
        if w == "d":
            for k in range(base // 128, (base + h) // 128):
                self.outd[pl.ds(k, 96, stride=n), :] = self.find[:, 128 * k : 128 * (k + 1)]
            return
        for plane in range(2):
            for k in range(h // 128):
                lc = base // 2 + 128 * k
                own = self.FIN[w][pl.ds(mult(self.c * 24, 8), 24), lc : lc + 128]
                other = self.FR[w][:, lc : lc + 128]
                val = jnp.where(self.c == plane, own, other)
                self.OUT[w][pl.ds((base + plane * h) // 128 + k, 24, stride=n), :] = val

    def do_gv0(self):
        self.store_vector_grads()
        self.send(self.gvb.at[:, 1 - self.y], self.gvy, self.ypeer, "gy", "gy")

    def do_gv1(self):
        self.arrived("gy", self.gvy)
        for zi in range(4):
            self.gvb[zi, self.y] = self.gvb[zi, self.y] + self.gvy[zi]
        for j in range(3):
            src = self.gvb.at[lax.rem(self.z + j + 1, 4), self.y]
            self.send(src, self.gvz.at[j], self.zpeers[j], "gz", "gz")

    def do_gv2(self):
        self.arrived("gz", self.gvz)
        self.gvs[...] = self.gvb[self.z, self.y] + self.gvz[0] + self.gvz[1] + self.gvz[2]
        for j in range(3):
            self.send(self.gvs, self.gv4.at[j], self.speers[j], "g4", "g4")

    def do_gv3(self):
        self.arrived("g4", self.gv4)
        self.outv[...] = self.gvs[...] + self.gv4[0] + self.gv4[1] + self.gv4[2]


    def do_masks(self):
        self.make_masks()

    def do_pickX(self):
        self.arrived("in", self.xs.at[:, 0:384])
        self.in_own.wait()
        self.pick(self.xs, self.xm)

    def do_projK(self):
        self.need_weight("q", D)
        self.project(D, self.ks, None, False)

    def do_projV(self):
        self.need_weight("q", 2 * D)
        self.project(2 * D, self.vs, BV, False)

    def do_projQ(self):
        self.need_weight("q", 0)
        self.project(0, self.qs, BQ, True)
        self.pick(self.qs, self.qm)

    def do_att(self, part):
        step = 12 // ATT_PARTS
        self.attend(part * step, part * step + step)

    def do_branch(self):
        self.need_weight("o")
        self.pick(self.qs, self.am)
        self.marked_branch()

    def do_up(self, fb):
        self.need_weight("u", fb * D)
        self.marked_up(fb)

    def do_down(self, name):
        self.need(name)
        self.marked_down(CHUNKS[name][1], CHUNKS[name][2])

    def do_sback(self):
        self.second_back()

    def do_gd(self):
        self.grad_down()

    def do_iback(self):
        self.inner_back()

    def do_gu(self, fb):
        self.grad_up(fb)

    def do_fback(self):
        self.first_back()

    def do_go(self):
        self.grad_out()

    def do_ab(self, part):
        self.attend_back(4 * part, 4 * part + 4)

    def do_inb(self):
        self.input_back()

    def do_gq(self, name):
        if not self.released:
            self.released = True
            self.release_gather()
        self.grad_qkv(CHUNKS[name][1])

    def do_fin(self, tile):
        self.finish_rows(tile)

    def do_end(self):
        self.arrived("ig", self.out_ig.at[0:6])
        for seq in range(NSEQ):
            self.arrived("out%d" % seq, self.out_rows.at[0:3])
        for copy in self.waits:
            copy.wait()
        self.finish()


def linked_kernel(*refs):
    k = Links(dict(zip(LINKED_NAMES, refs)))
    k.do_start()
    k.do_ag(U3, 0)
    k.do_ag(Q, 0)
    k.do_ag(K, 0)
    k.do_ag(Q, 1)
    k.do_ag(U1, 0)
    k.do_ag(U3, 1)
    k.do_ag(K, 1)
    k.do_ag(U0, 0)
    k.do_ag(U2, 0)
    k.do_ag(V, 0)
    k.do_ag(O, 0)
    k.do_ag(D0, 0)
    k.do_ag(U1, 1)
    k.do_ag(V, 1)
    k.do_ag(Q, 2)
    k.do_vec0()
    k.do_masks()
    k.do_ag(U0, 1)
    k.do_ag(O, 1)
    k.do_ag(D2, 0)
    k.do_ag(D1, 0)
    k.do_ag(U2, 1)
    k.do_ag(D0, 1)
    k.do_vec1()
    k.do_pickX()
    k.do_ag(V, 2)
    k.do_ag(K, 2)
    k.do_ag(O, 2)
    k.do_ag(Q, 3)
    k.do_ag(U3, 2)
    k.do_ag(D2, 1)
    k.do_vec()
    k.do_projQ()
    k.do_ag(D1, 1)
    k.do_ag(U2, 2)
    k.do_ag(D0, 2)
    k.do_ag(U0, 2)
    k.do_ag(V, 3)
    k.do_projV()
    k.do_ag(K, 3)
    k.do_projK()
    k.do_ag(U1, 2)
    k.do_ag(O, 3)
    k.do_att(0)
    k.do_ag(U3, 3)
    k.do_ag(D2, 2)
    k.do_tog()
    k.do_att(1)
    k.do_att(2)
    k.do_att(3)
    k.do_att(4)
    k.do_ag(U0, 3)
    k.do_ag(D1, 2)
    k.do_att(5)
    k.do_branch()
    k.do_up(3)
    k.do_ag(U1, 3)
    k.do_up(0)
    k.do_ag(D2, 3)
    k.do_ag(U2, 3)
    k.do_ag(D0, 3)
    k.do_up(1)
    k.do_up(2)
    k.do_down(D2)
    k.do_down(D0)
    k.do_ag(D1, 3)
    k.do_down(D1)
    k.do_pickC()
    k.do_sback()
    k.do_gd()
    k.do_rs(D0, -1)
    k.do_rs(D2, -1)
    k.do_rs(D1, -1)
    k.do_iback()
    k.do_gu(0)
    k.do_rs(U0, -1)
    k.do_rs(D0, 0)
    k.do_rs(D1, 0)
    k.do_gu(3)
    k.do_rs(U3, -1)
    k.do_fback()
    k.do_rs(D2, 0)
    k.do_go()
    k.do_rs(O, -1)
    k.do_rs(U3, 0)
    k.do_rs(U0, 0)
    k.do_gu(1)
    k.do_rs(U1, -1)
    k.do_ab(0)
    k.do_rs(O, 0)
    k.do_rs(U1, 0)
    k.do_rs(D0, 1)
    k.do_ab(1)
    k.do_rs(D2, 1)
    k.do_ab(2)
    k.do_rs(U3, 1)
    k.do_inb()
    k.do_igout()
    k.do_rs(O, 1)
    k.do_rs(U0, 1)
    k.do_gq(K)
    k.do_rs(K, -1)
    k.do_gq(Q)
    k.do_rs(Q, -1)
    k.do_rs(D1, 1)
    k.do_rs(U1, 1)
    k.do_gu(2)
    k.do_rs(U0, 2)
    k.do_fin(0)
    k.do_rs(Q, 0)
    k.do_rs(D2, 2)
    k.do_rs(D1, 2)
    k.do_rs(K, 0)
    k.do_rs(U2, -1)
    k.do_gq(V)
    k.do_rs(V, -1)
    k.do_rs(O, 2)
    k.do_fin(1)
    k.do_rs(V, 0)
    k.do_out(0)
    k.do_gv0()
    k.do_rs(U0, 3)
    k.do_rs(U2, 0)
    k.do_rs(U1, 2)
    k.do_fin(2)
    k.do_rs(K, 1)
    k.do_fin(3)
    k.do_rs(D0, 2)
    k.do_rs(V, 1)
    k.do_gv1()
    k.do_rs(K, 2)
    k.do_rs(U2, 1)
    k.do_rs(Q, 1)
    k.do_gv2()
    k.do_rs(U3, 2)
    k.do_rs(D2, 3)
    k.do_rs(D2, 4)
    k.do_rs(Q, 2)
    k.do_rs(O, 3)
    k.do_rs(O, 4)
    k.do_rs(V, 2)
    k.do_out(1)
    k.do_rs(D1, 3)
    k.do_rs(D1, 4)
    k.do_rs(D0, 3)
    k.do_rs(D0, 4)
    k.do_rs(U3, 3)
    k.do_rs(U2, 2)
    k.do_rs(U1, 3)
    k.do_rs(U3, 4)
    k.do_rs(K, 3)
    k.do_rs(K, 4)
    k.do_rs(U1, 4)
    k.do_rs(Q, 3)
    k.do_rs(Q, 4)
    k.do_gv3()
    k.do_rs(U0, 4)
    k.do_rs(V, 3)
    k.do_rs(V, 4)
    k.do_rs(U2, 3)
    k.do_rs(U2, 4)
    k.do_end()

def plain_kernel(*refs):
    k = Layer(dict(zip(PLAIN_NAMES, refs)))
    pairs = [(k.inp, k.xs), (k.outg, k.ogl), (k.inq, k.wq), (k.ino, k.wo), (k.inu, k.wu), (k.ind, k.wd)]
    copies = [pltpu.make_async_copy(src, dst, k.lsem.at[n]) for n, (src, dst) in enumerate(pairs)]
    for copy in copies:
        copy.start()
    for copy in copies:
        copy.wait()
    k.make_masks()
    k.load_vector()
    k.pick(k.xs, k.xm)
    k.project(D, k.ks, None, False)
    k.project(2 * D, k.vs, BV, False)
    k.project(0, k.qs, BQ, True)
    k.pick(k.qs, k.qm)
    k.attend(0, 12)
    k.pick(k.qs, k.am)
    k.marked_branch()
    for fb in range(4):
        k.marked_up(fb)
    k.pick(k.ogl, k.cm)
    for first in (0, 256, 512):
        k.marked_down(first, 256)
    k.second_back()
    k.grad_down()
    k.inner_back()
    for fb in range(4):
        k.grad_up(fb)
    k.first_back()
    k.grad_out()
    k.attend_back(0, 12)
    k.input_back()
    k.store_vector_grads()
    for first in (D, 2 * D, 0):
        k.grad_qkv(first)
    for tile in range(4):
        k.finish_rows(tile)
    for seq in range(NSEQ):
        for half in range(2):
            k.ogl[seq, 256 * half : 256 * half + 256] = k.og[half, seq]
    pairs = [(k.qs, k.out_rows), (k.ogl, k.out_ig), (k.wq, k.outq), (k.go, k.outo), (k.gu, k.outu), (k.gd, k.outd)]
    copies = [pltpu.make_async_copy(src, dst, k.lsem.at[n]) for n, (src, dst) in enumerate(pairs)]
    for copy in copies:
        copy.start()
    for copy in copies:
        copy.wait()
    k.outv[...] = k.gvb[...]


def wshape(w):
    return (4, 2, 2, PIECE[w], COLS[w])


COMMON_SCRATCH = [
    ("wq", wshape("q"), BF),
    ("wo", wshape("o"), BF),
    ("wu", wshape("u"), BF),
    ("wd", wshape("d"), BF),
    ("xs", (NSEQ, LEN, D), BF),
    ("og", (2, NSEQ, 256, D), BF),
    ("qs", (NSEQ, LEN, D), BF),
    ("ks", (NSEQ, LEN, D), BF),
    ("vs", (NSEQ, LEN, D), BF),
    ("sel", (2 * NSEQ, SLOTS, LEN), BF),
    ("kmask", (NSEQ, LEN, 128), F32),
    ("vrow", (1, VEC), F32),
    ("gvrow", (1, VEC), F32),
    ("gvb", (4, 2, 16, 128), F32),
    ("xm", (MROWS, D), BF),
    ("am", (MROWS, D), BF),
    ("qm", (MROWS, D), BF),
    ("cm", (MROWS, D), BF),
    ("low", (MROWS, D), BF),
    ("g2", (MROWS, D), BF),
    ("ga", (MROWS, D), BF),
    ("gq", (MROWS, D), BF),
    ("f0", (MROWS, D), F32),
    ("f1", (MROWS, D), F32),
    ("f3", (MROWS, D), F32),
    ("sc1", (MROWS, 128), F32),
    ("act", (MROWS, FF), BF),
    ("dgl", (MROWS, FF), F32),
    ("gd", wshape("d"), BF),
    ("gu", wshape("u"), BF),
    ("go", wshape("o"), BF),
    ("tlow", (256, D), BF),
    ("tacc", (256, D), F32),
]


def linked_scratch():
    out = list(COMMON_SCRATCH)
    out += [("vb", (4, 2, 16, 128), F32), ("v4", (3, 16, 128), F32)]
    for w in ("q", "o", "u"):
        out += [("s24" + w, (24, COLS[w]), F32), ("sib" + w, (24, COLS[w] // 2), F32)]
    for w in ("q", "o", "u", "d"):
        rows = 96 if w == "d" else 48
        half = D if w == "d" else COLS[w] // 2
        out.append(("fin" + w, (rows, half), F32))
        if w != "d":
            out.append(("fr" + w, (24, half), F32))
    for name, (w, _, h, _, order) in CHUNKS.items():
        rows = 96 if w == "d" else 48
        shape = dict(FULL)
        out.append(("rt" + name, (4, 2, 2, rows, h), BF))
        for stage, axis in enumerate(order):
            shape[axis] = 3 if axis == "z" else 1
            out.append(("r%d" % stage + name, (shape["z"], shape["y"], shape["x"], rows, h), BF))
            shape[axis] = 1
    out += [
        ("cmx", (MROWS, D), BF),
        ("cmr", (MROWS, D), BF),
        ("gvy", (4, 16, 128), F32),
        ("gvz", (3, 16, 128), F32),
        ("gvs", (16, 128), F32),
        ("gv4", (3, 16, 128), F32),
    ]
    return out


LINKED_SCRATCH = linked_scratch()
LINKED_INS = ["lengths", "spans", "inp", "outg", "fq", "fo", "fu", "fd", "vec_in"]
LINKED_OUTS = ["out_rows", "out_ig", "outq", "outo", "outu", "outd", "outv"]
LINKED_NAMES = LINKED_INS + LINKED_OUTS + [n for n, _, _ in LINKED_SCRATCH] + ["ssem", "rsem", "lsem"]
PLAIN_INS = ["lengths", "spans", "inp", "outg", "inq", "ino", "inu", "ind", "vb"]
PLAIN_SCRATCH = COMMON_SCRATCH + [("ogl", (NSEQ, LEN, D), BF)]
PLAIN_NAMES = PLAIN_INS + LINKED_OUTS + [n for n, _, _ in PLAIN_SCRATCH] + ["lsem"]

IN_VMEM = pl.BlockSpec(memory_space=pltpu.VMEM)
IN_SMEM = pl.BlockSpec(memory_space=pltpu.SMEM)
ANYWHERE = pl.BlockSpec(memory_space=pl.ANY)


def flat_shape(w):
    return (OWN_ROWS[w] * COLS[w] // 128, 128)


def linked_call(lengths, spans, inp, outg, flats, vec_in):
    outs = [jax.ShapeDtypeStruct((8, BLK, D), BF)] * 2
    outs += [jax.ShapeDtypeStruct(flat_shape(w), F32) for w in ("q", "o", "u", "d")]
    outs += [jax.ShapeDtypeStruct((16, 128), F32)]
    return pl.pallas_call(
        linked_kernel,
        out_shape=outs,
        in_specs=[IN_SMEM, IN_VMEM, ANYWHERE, ANYWHERE] + [IN_VMEM] * 5,
        out_specs=[ANYWHERE, ANYWHERE] + [IN_VMEM] * 5,
        scratch_shapes=[pltpu.VMEM(shape, dtype) for _, shape, dtype in LINKED_SCRATCH]
        + [pltpu.SemaphoreType.DMA((NSEND,)), pltpu.SemaphoreType.DMA((NRECV,)), pltpu.SemaphoreType.DMA((8,))],
        compiler_params=pltpu.CompilerParams(
            collective_id=0, has_side_effects=True, vmem_limit_bytes=64 * 2**20 - 2**16
        ),
        name="layer",
    )(lengths, spans, inp, outg, *flats, vec_in)


def plain_call(lengths, spans, inp, outg, weights, vb):
    outs = [jax.ShapeDtypeStruct((NSEQ, LEN, D), BF)] * 2
    outs += [jax.ShapeDtypeStruct(wshape(w), BF) for w in ("q", "o", "u", "d")]
    outs += [jax.ShapeDtypeStruct((4, 2, 16, 128), F32)]
    return pl.pallas_call(
        plain_kernel,
        out_shape=outs,
        in_specs=[IN_SMEM, IN_VMEM] + [ANYWHERE] * 6 + [IN_VMEM],
        out_specs=[ANYWHERE] * 6 + [IN_VMEM],
        scratch_shapes=[pltpu.VMEM(shape, dtype) for _, shape, dtype in PLAIN_SCRATCH]
        + [pltpu.SemaphoreType.DMA((8,))],
        compiler_params=pltpu.CompilerParams(vmem_limit_bytes=60 * 2**20),
        name="layer",
    )(lengths, spans, inp, outg, *weights, vb)


def adam_update(master, first_moment, second_moment, gradient, step_rate, decay_rate):
    new_first = FIRST_DECAY * first_moment + (1.0 - FIRST_DECAY) * gradient
    new_second = SECOND_DECAY * second_moment + (1.0 - SECOND_DECAY) * gradient * gradient
    first_hat = new_first / (1.0 - FIRST_DECAY**STEP)
    second_hat = new_second / (1.0 - SECOND_DECAY**STEP)
    new_master = master - step_rate * (
        first_hat / (jnp.sqrt(second_hat) + ADAM_EPS) + decay_rate * master
    )
    return (new_master, new_first, new_second, new_master.astype(jnp.bfloat16))


RATES = (1.6 / math.sqrt(D), 1.6 / math.sqrt(D), 1.6 / math.sqrt(D), 1.6 / math.sqrt(FF))


def adam_kernel(*refs):
    for n in range(4):
        grad, master, first, second = (refs[4 * n + m][...] for m in range(4))
        for out, value in zip(refs[16 + 4 * n : 20 + 4 * n], adam_update(master, first, second, grad, RATES[n], 0.01)):
            out[...] = value


def adam_call(groups):
    steps = 3
    specs, outs, out_specs, flat = [], [], [], []
    for group in groups:
        rows = group[0].shape[0]
        spec = pl.BlockSpec((rows // steps, 128), lambda i: (i, 0))
        specs += [spec] * 4
        out_specs += [spec] * 4
        outs += [jax.ShapeDtypeStruct((rows, 128), F32)] * 3 + [jax.ShapeDtypeStruct((rows, 128), BF)]
        flat += list(group)
    new = pl.pallas_call(
        adam_kernel,
        out_shape=outs,
        grid=(steps,),
        in_specs=specs,
        out_specs=out_specs,
        compiler_params=pltpu.CompilerParams(vmem_limit_bytes=32 * 2**20),
        name="adam",
    )(*flat)
    return [tuple(a.reshape(-1) for a in new[4 * n : 4 * n + 4]) for n in range(4)]


def on_device(
    inputs,
    out_grad,
    lengths,
    word_spans,
    qkv_weight,
    qkv_first,
    qkv_second,
    out_weight,
    out_first,
    out_second,
    up_weight,
    up_first,
    up_second,
    down_weight,
    down_first,
    down_second,
    vec_weight,
    vec_first,
    vec_second,
):
    groups = [
        (qkv_weight, qkv_first, qkv_second),
        (out_weight, out_first, out_second),
        (up_weight, up_first, up_second),
        (down_weight, down_first, down_second),
    ]
    everywhere = ("batch", "seq")
    if lax.axis_size("batch") == 8 and lax.axis_size("seq") == 4:
        place = lax.axis_index("seq")
        share = vec_weight.shape[0]
        vec_in = lax.dynamic_update_slice(jnp.zeros((16 * 128,), F32), vec_weight, (share * place,)).reshape(16, 128)
        flats = [group[0].reshape(-1, 128) for group in groups]
        rows, in_grad, *sums, vec_sum = linked_call(lengths, word_spans, inputs, out_grad, flats, vec_in)
        vec_grad = lax.dynamic_slice(vec_sum.reshape(-1), (share * place,), (share,))
        news = adam_call([(g,) + tuple(a.reshape(-1, 128) for a in group) for g, group in zip(sums, groups)])
        in_grad = in_grad.astype(F32)
    else:
        weights = [
            lax.all_gather(group[0].astype(BF), everywhere, axis=0, tiled=True).reshape(wshape(w))
            for w, group in zip("qoud", groups)
        ]
        vector = lax.all_gather(vec_weight.astype(BF), everywhere, axis=0, tiled=True).astype(F32)
        vb = jnp.pad(vector.reshape(4, 2, VROWS, 128), ((0, 0), (0, 0), (0, 16 - VROWS), (0, 0)))
        own = lax.axis_index("seq") * NSEQ
        xs, og = (
            lax.all_to_all(a, "seq", split_axis=0, concat_axis=1, tiled=True) for a in (inputs, out_grad)
        )
        rows, in_grad, *grads, gvb = plain_call(lengths, word_spans, xs, og, weights, vb)
        rows, in_grad = (
            lax.all_to_all(a, "seq", split_axis=1, concat_axis=0, tiled=True) for a in (rows, in_grad)
        )
        in_grad = in_grad.astype(F32)
        sums = [
            lax.psum_scatter(g.astype(F32).reshape(-1), everywhere, scatter_dimension=0, tiled=True) for g in grads
        ]
        vec_grad = lax.psum_scatter(
            gvb[:, :, :VROWS].reshape(-1), everywhere, scatter_dimension=0, tiled=True
        )
        news = [
            adam_update(master, first, second, g, rate, 0.01)
            for (master, first, second), g, rate in zip(groups, sums, RATES)
        ]
    vec_new = adam_update(vec_weight, vec_first, vec_second, vec_grad, 0.4, 0.0)
    flat = [array for new in news for array in new]
    return (rows, in_grad, *flat, *vec_new)


def solution(mesh):
    owned = P(("batch", "seq"))
    rows = P("batch", "seq", None)
    in_specs = (rows, rows, P("batch"), P("batch", None, None)) + (owned,) * 15
    out_specs = (rows, rows) + (owned,) * 20
    return jax.shard_map(on_device, mesh=mesh, in_specs=in_specs, out_specs=out_specs, check_vma=False)
```

```python
import math

import jax
import jax.numpy as jnp
from jax import lax
from jax.experimental import pallas as pl
from jax.experimental.pallas import tpu as pltpu
from jax.sharding import PartitionSpec as P

D = 768
HDIM = 64
FF = 3072
STEP = 10
LEN = 512
BLK = 128
SLOTS = 128
NSEQ = 2
ROWS = NSEQ * LEN
MROWS = NSEQ * SLOTS
VEC = 9216
VROWS = 9

NORM_EPS = 1e-12
ADAM_EPS = 1e-08
FIRST_DECAY = 0.9
SECOND_DECAY = 0.999
NEG_LARGE = -1000000000.0

BF, F32 = jnp.bfloat16, jnp.float32
MESH = pl.DeviceIdType.MESH
ALL = slice(None)

BQ, BV, BO, G1, S1, BU, BD, G2, S2 = 0, 768, 1536, 2304, 3072, 3840, 6912, 7680, 8448

K = "K"
V = "V"
Q = "Q"
O = "o"
U0 = "u0"
U1 = "u1"
U2 = "u2"
U3 = "u3"
D0 = "d0"
D1 = "d1"
D2 = "d2"
CHUNKS = {
    K: ("q", 768, 384, "zyx", "yxz"),
    V: ("q", 1536, 384, "zxy", "yxz"),
    Q: ("q", 0, 384, "zxy", "zyx"),
    O: ("o", 0, 384, "zyx", "yxz"),
    U0: ("u", 0, 384, "yzx", "yxz"),
    U1: ("u", 768, 384, "zyx", "yzx"),
    U2: ("u", 1536, 384, "yxz", "yxz"),
    U3: ("u", 2304, 384, "zxy", "xyz"),
    D0: ("d", 0, 256, "xzy", "xzy"),
    D1: ("d", 256, 256, "zxy", "zyx"),
    D2: ("d", 512, 256, "xzy", "yxz"),
}
COLS = {"q": 3 * D, "o": D, "u": FF, "d": D}
PIECE = {"q": 48, "o": 48, "u": 48, "d": 192}
OWN_ROWS = {"q": 24, "o": 24, "u": 24, "d": 96}
FULL = {"z": 4, "y": 2, "x": 2}
ATT_PARTS = 6
NSEND = 60
NRECV = 120


def mult(value, step=128):
    return pl.multiple_of(value, step)


def dot(a, b):
    return lax.dot_general(a, b, (((1,), (0,)), ((), ())), preferred_element_type=F32)


def dot_nt(a, b):
    return lax.dot_general(a, b, (((1,), (1,)), ((), ())), preferred_element_type=F32)


def dot_tn(a, b):
    return lax.dot_general(a, b, (((0,), (0,)), ((), ())), preferred_element_type=F32)


def normalize(rows):
    center = rows - jnp.sum(rows, axis=-1, keepdims=True) * (1.0 / D)
    spread = jnp.sum(center * center, axis=-1, keepdims=True) * (1.0 / D)
    scale = lax.rsqrt(spread + NORM_EPS)
    return center * scale, scale


def norm_back(grad, gain, hat, scale):
    cg = grad * gain
    mean_one = jnp.sum(cg, axis=-1, keepdims=True) * (1.0 / D)
    mean_hat = jnp.sum(cg * hat, axis=-1, keepdims=True) * (1.0 / D)
    return scale * (cg - mean_one - hat * mean_hat)


def normal_cdf(v):
    return 0.5 * (1.0 + lax.erf(v * math.sqrt(0.5)))


def row_sum(rows):
    return jnp.sum(rows, axis=0, keepdims=True)


class Layer:
    def __init__(self, refs):
        self.__dict__.update(refs)
        self.b = lax.axis_index("batch")
        self.s = lax.axis_index("seq")


    def vec(self, first, count):
        return self.vrow[0:1, first : first + count]

    def vec_at(self, first, block, count):
        return self.vrow[0:1, pl.ds(mult(first + block * count), count)]

    def wcols(self, ref, first, count):
        return ref[:, :, :, :, pl.ds(first, count)].reshape(D, count)

    def load_vector(self):
        for r in range(VEC // 128):
            blk = r // VROWS
            line = self.vb[blk // 2, blk % 2, r % VROWS : r % VROWS + 1, :]
            self.vrow[0:1, 128 * r : 128 * r + 128] = line.astype(BF).astype(F32)

    def store_vector_grads(self):
        for r in range(VEC // 128):
            blk = r // VROWS
            self.gvb[blk // 2, blk % 2, r % VROWS : r % VROWS + 1, :] = self.gvrow[0:1, 128 * r : 128 * r + 128]


    def make_masks(self):
        below = lax.broadcasted_iota(jnp.int32, (LEN, 128), 0)
        lane = lax.broadcasted_iota(jnp.int32, (LEN, 128), 1)
        upper = (
            lax.broadcasted_iota(jnp.int32, (LEN, LEN), 0) < lax.broadcasted_iota(jnp.int32, (LEN, LEN), 1)
        ).astype(F32).astype(BF)
        slot = lax.broadcasted_iota(jnp.int32, (SLOTS, LEN), 0).astype(F32)
        for i in range(NSEQ):
            length = self.lengths[self.s * NSEQ + i]
            self.kmask[i] = jnp.where((below >= length) & (lane == 0), NEG_LARGE, 0.0).astype(BF)
        for i, number in enumerate(self.mask_rows()):
            starts = self.spans[number, :, 0:1]
            counts = self.spans[number, :, 1:2]
            spot = lax.broadcasted_iota(jnp.int32, (32, LEN), 1)
            inside = jnp.where((spot >= starts) & (spot < starts + counts), 1.0, 0.0)
            marked = jnp.max(inside, axis=0, keepdims=True)
            rank = dot(jnp.broadcast_to(marked, (16, LEN)).astype(BF), upper)[0:1]
            rank = jnp.where(marked > 0.5, rank, -1.0)
            self.sel[i] = jnp.where(slot == rank, 1.0, 0.0).astype(BF)

    def mask_rows(self):
        return [self.s * NSEQ + i for i in range(NSEQ)]


    def project(self, first, dst, bias, scale):
        def body(i, _):
            seq, blk = lax.div(i, 3), lax.rem(i, 3)
            acc = dot(self.xs[seq], self.wcols(self.wq, mult(first + blk * 256), 256))
            if bias is not None:
                acc = acc + self.vrow[0:1, pl.ds(mult(bias + blk * 256), 256)]
            if scale:
                acc = acc * (1.0 / math.sqrt(HDIM))
            dst[seq, :, pl.ds(mult(blk * 256), 256)] = acc.astype(BF)
            return 0

        lax.fori_loop(0, 3 * NSEQ, body, 0)

    def pick(self, src, dst):
        for i in range(NSEQ):
            dst[SLOTS * i : SLOTS * (i + 1)] = dot(self.sel[i], src[i]).astype(BF)

    def masked_keys(self, seq, cols):
        return jnp.concatenate([self.ks[seq, :, cols], self.kmask[seq]], axis=1)

    def both_heads(self, rows):
        r = rows.astype(F32)
        low = lax.broadcasted_iota(jnp.int32, r.shape, 1) < HDIM
        return jnp.concatenate([jnp.where(low, r, 0.0), jnp.where(low, 0.0, r)], axis=0).astype(BF)

    def with_mark(self, rows):
        lane = lax.broadcasted_iota(jnp.int32, rows.shape, 1)
        return jnp.concatenate([rows, jnp.where(lane == 0, 1.0, 0.0).astype(BF)], axis=1)

    def attend(self, lo, hi):
        low = lax.broadcasted_iota(jnp.int32, (256, 128), 1) < HDIM

        def body(i, _):
            seq = lax.div(i, 6)
            cols = pl.ds(mult(lax.rem(i, 6) * 128), 128)
            keys = self.masked_keys(seq, cols)
            v = jnp.concatenate([self.vs[seq, :, cols], jnp.ones((LEN, 128), BF)], axis=1)
            for rt in range(2):
                rows = slice(256 * rt, 256 * rt + 256)
                q = self.both_heads(self.qs[seq, rows, cols])
                outs = []
                for e in range(2):
                    scores = dot_nt(self.with_mark(q[256 * e : 256 * e + 256]), keys)
                    p = jnp.exp(scores - jnp.max(scores, axis=-1, keepdims=True))
                    mixed = dot(p.astype(BF), v)
                    outs.append(mixed[:, :128] * (1.0 / mixed[:, 128:]))
                self.qs[seq, rows, cols] = jnp.where(low, outs[0], outs[1]).astype(BF)
            return 0

        lax.fori_loop(lo, hi, body, 0)

    def marked_branch(self):
        r = dot(self.am[...], self.wcols(self.wo, 0, D)) + self.vec(BO, D) + self.xm[...].astype(F32)
        hat, scale = normalize(r)
        self.f1[...] = hat
        self.sc1[...] = jnp.broadcast_to(scale, (MROWS, 128))
        first = hat * self.vec(G1, D) + self.vec(S1, D)
        self.f0[...] = first
        self.low[...] = first.astype(BF)

    def marked_up(self, fb):
        def body(j, _):
            cols = pl.ds(mult(fb * D + j * 256), 256)
            v = dot(self.low[...], self.wcols(self.wu, mult(fb * D + j * 256), 256))
            v = v + self.vrow[0:1, pl.ds(mult(BU + fb * D + j * 256), 256)]
            cdf = normal_cdf(v)
            self.act[:, cols] = (v * cdf).astype(BF)
            self.dgl[:, cols] = cdf + v * (jnp.exp(-0.5 * v * v) * (1.0 / math.sqrt(2.0 * math.pi)))
            return 0

        lax.fori_loop(0, 3, body, 0)

    def marked_down(self, first, count):
        w = self.wd[:, :, :, :, first : first + count].reshape(FF, count)
        self.f3[:, first : first + count] = dot(self.act[...], w)

    def second_back(self):
        r = self.f0[...] + self.f3[...] + self.vec(BD, D)
        hat, scale = normalize(r)
        cot = self.cm[...].astype(F32)
        self.gvrow[0:1, S2 : S2 + D] = row_sum(cot)
        self.gvrow[0:1, G2 : G2 + D] = row_sum(cot * hat)
        g_two = norm_back(cot, self.vec(G2, D), hat, scale)
        self.f0[...] = g_two
        g_low = g_two.astype(BF)
        self.g2[...] = g_low
        self.gvrow[0:1, BD : BD + D] = row_sum(g_low.astype(F32))

    def grad_down(self):
        def body(i, _):
            zi, yi = lax.div(i, 2), lax.rem(i, 2)
            g = dot_tn(self.act[:, pl.ds(mult(i * 384), 384)], self.g2[...])
            self.gd[zi, yi] = g.astype(BF).reshape(2, 192, D)
            return 0

        lax.fori_loop(0, 8, body, 0)

    def inner_back(self):
        def body(i, _):
            zi, yi = lax.div(i, 2), lax.rem(i, 2)
            cols = pl.ds(mult(i * 384), 384)
            g = dot_nt(self.g2[...], self.wd[zi, yi].reshape(384, D)) * self.dgl[:, cols]
            g = g.astype(BF)
            self.act[:, cols] = g
            self.gvrow[0:1, pl.ds(mult(BU + i * 384), 384)] = row_sum(g.astype(F32))
            return 0

        lax.fori_loop(0, 8, body, 0)

    def outer(self, left, right, dst, first):
        def body(m, _):
            g = dot_tn(left[:, pl.ds(mult(m * 384), 384)], right)
            dst[pl.ds(m * 2, 2), :, :, :, first : first + D] = g.astype(BF).reshape(2, 2, 2, 48, D)
            return 0

        lax.fori_loop(0, 2, body, 0)

    def grad_up(self, fb):
        self.outer(self.low, self.act[:, fb * D : fb * D + D], self.gu, fb * D)

    def first_back(self):
        def body(fb, _):
            w = self.wcols(self.wu, mult(fb * D), D)
            self.f0[...] += dot_nt(self.act[:, pl.ds(mult(fb * D), D)], w)
            return 0

        lax.fori_loop(0, 4, body, 0)
        grad = self.f0[...]
        hat = self.f1[...]
        self.gvrow[0:1, S1 : S1 + D] = row_sum(grad)
        self.gvrow[0:1, G1 : G1 + D] = row_sum(grad * hat)
        g_one = norm_back(grad, self.vec(G1, D), hat, self.sc1[:, 0:1])
        self.f0[...] = g_one
        g_low = g_one.astype(BF)
        self.g2[...] = g_low
        self.gvrow[0:1, BO : BO + D] = row_sum(g_low.astype(F32))
        self.ga[...] = dot_nt(g_low, self.wcols(self.wo, 0, D)).astype(BF)

    def grad_out(self):
        self.outer(self.am, self.g2[...], self.go, 0)

    def attend_back(self, lo, hi):
        low = lax.broadcasted_iota(jnp.int32, (SLOTS, 128), 1) < HDIM

        def body(i, _):
            seq, hp = lax.div(i, 6), lax.rem(i, 6)
            cols = pl.ds(mult(hp * 128), 128)
            rows = pl.ds(mult(seq * SLOTS), SLOTS)
            q = self.both_heads(self.qm[rows, cols])
            ga = self.both_heads(self.ga[rows, cols])
            scores = dot_nt(self.with_mark(q), self.masked_keys(seq, cols))
            p = jnp.exp(scores - jnp.max(scores, axis=-1, keepdims=True))
            p = p * (1.0 / jnp.sum(p, axis=-1, keepdims=True))
            dp = dot_nt(ga, self.vs[seq, :, cols])
            gs = p * (dp - jnp.sum(p * dp, axis=-1, keepdims=True))
            gs = gs.astype(BF)
            gq = dot(gs, self.ks[seq, :, cols])
            gk = dot_tn(gs, q)
            gv = dot_tn(p.astype(BF), ga)
            gql = jnp.where(low, gq[:SLOTS], gq[SLOTS:]).astype(BF).astype(F32) * (1.0 / math.sqrt(HDIM))
            self.gq[rows, cols] = gql.astype(BF)
            self.ks[seq, :, cols] = gk.astype(BF)
            self.vs[seq, :, cols] = gv.astype(BF)
            return 0

        lax.fori_loop(lo, hi, body, 0)

    def input_back(self):
        self.gvrow[0:1, BQ : BQ + D] = row_sum(self.gq[...].astype(F32))
        self.gvrow[0:1, BV : BV + D] = row_sum(self.vs[0].astype(F32)) + row_sum(self.vs[1].astype(F32))
        t = self.f0[...] + dot_nt(self.gq[...], self.wcols(self.wq, 0, D))
        hi = t.astype(BF)
        self.ga[...] = hi
        self.cm[...] = (t - hi.astype(F32)).astype(BF)

        def body(i, _):
            seq, half = lax.div(i, 2), lax.rem(i, 2)
            rows = pl.ds(mult(half * 256, 256), 256)
            slots = pl.ds(mult(seq * SLOTS), SLOTS)
            acc = dot_nt(self.ks[seq, rows], self.wcols(self.wq, D, D))
            acc = acc + dot_nt(self.vs[seq, rows], self.wcols(self.wq, 2 * D, D))
            s = self.sel[seq, :, rows]
            acc = acc + (dot_tn(s, self.ga[slots]) + dot_tn(s, self.cm[slots]))
            self.og[half, seq] = acc.astype(BF)
            return 0

        lax.fori_loop(0, 4, body, 0)

    def grad_qkv(self, first):
        if first == 0:
            self.outer(self.xm, self.gq[...], self.wq, 0)
            return
        src = self.ks if first == D else self.vs

        def body(m, _):
            cols = pl.ds(mult(m * 384), 384)
            g = dot_tn(self.xs[:, :, cols].reshape(ROWS, 384), src[...].reshape(ROWS, D))
            self.wq[pl.ds(m * 2, 2), :, :, :, first : first + D] = g.astype(BF).reshape(2, 2, 2, 48, D)
            return 0

        lax.fori_loop(0, 2, body, 0)

    def finish_rows(self, tile):
        seq, rows = tile // 2, slice(256 * (tile % 2), 256 * (tile % 2) + 256)
        r = dot(self.qs[seq, rows], self.wcols(self.wo, 0, D)) + self.vec(BO, D) + self.xs[seq, rows].astype(F32)
        hat, _ = normalize(r)
        first = hat * self.vec(G1, D) + self.vec(S1, D)
        self.tacc[...] = first + self.vec(BD, D)
        self.tlow[...] = first.astype(BF)

        low = self.tlow[...]
        half = FF // 8

        def up(j):
            first = j * half
            return dot(low, self.wcols(self.wu, first, half)) + self.vec(BU + first, half)

        acc, v = self.tacc[...], up(0)
        for j in range(8):
            a = (v * normal_cdf(v)).astype(BF)
            if j < 7:
                v = up(j + 1)
            acc = acc + dot(a, self.wd[j // 2, j % 2].reshape(half, D))
        self.tacc[...] = acc
        hat, _ = normalize(self.tacc[...])
        out = hat * self.vec(G2, D) + self.vec(S2, D)
        place = lax.broadcasted_iota(jnp.int32, (256, D), 0) + 256 * (tile % 2)
        out = jnp.where(place < self.lengths[self.s * NSEQ + seq], out, 0.0)
        self.qs[seq, rows] = out.astype(BF)


class Links(Layer):
    def __init__(self, refs):
        super().__init__(refs)
        b, s = self.b, self.s
        self.z, self.y = lax.div(b, 2), lax.rem(b, 2)
        self.x, self.c = lax.div(s, 2), lax.rem(s, 2)
        self.zpeers = [(lax.rem(self.z + j, 4) * 2 + self.y, s) for j in (1, 2, 3)]
        self.zfrom = [lax.rem(self.z + 4 - j, 4) for j in (1, 2, 3)]
        self.xpeer = (b, (1 - self.x) * 2 + self.c)
        self.ypeer = (self.z * 2 + 1 - self.y, s)
        self.twin = (b, self.x * 2 + 1 - self.c)
        self.speers = [(b, lax.rem(s + j, 4)) for j in (1, 2, 3)]
        self.send_ids, self.recv_ids = {}, {}
        self.released = False
        self.W = {"q": self.wq, "o": self.wo, "u": self.wu, "d": self.wd}
        self.G = {"q": self.wq, "o": self.go, "u": self.gu, "d": self.gd}

    def greet(self):
        sem = pltpu.get_barrier_semaphore()
        peers = self.zpeers + [self.ypeer] + self.speers
        for peer in peers:
            pl.semaphore_signal(sem, inc=1, device_id=peer, device_id_type=MESH)
        pl.semaphore_wait(sem, len(peers))

    def send(self, src, dst, peer, recv, sent):
        ours = self.send_ids.setdefault(sent, len(self.send_ids))
        theirs = self.recv_ids.setdefault(recv, len(self.recv_ids))
        assert ours < NSEND and theirs < NRECV
        pltpu.make_async_remote_copy(
            src_ref=src,
            dst_ref=dst,
            send_sem=self.ssem.at[ours],
            recv_sem=self.rsem.at[theirs],
            device_id=peer,
            device_id_type=MESH,
        ).start()

    def arrived(self, recv, alike):
        pltpu.make_async_copy(alike, alike, self.rsem.at[self.recv_ids[recv]]).wait()

    def left(self, sent, alike):
        pltpu.make_async_copy(alike, alike, self.ssem.at[self.send_ids[sent]]).wait()

    def fifteen(self, name):
        return self.wu.at[0:4, 0:1, 0:1, :, 0:1920] if CHUNKS[name][0] == "d" else self.wu.at[0:3, 0:1, 0:1, :, 0 : 5 * CHUNKS[name][2]]

    def local(self, src, dst, number):
        copy = pltpu.make_async_copy(src, dst, self.lsem.at[number])
        copy.start()
        return copy

    def release_gather(self):
        for name in CHUNKS:
            self.left("g" + name, self.fifteen(name))
            self.left("m" + name, self.view(self.W, name, ALL, ALL, ALL, self.c))

    def finish(self):
        for name in CHUNKS:
            self.left("t" + name, self.__dict__["rt" + name])
            self.left("s" + name, self.fifteen(name))
        self.left("f", self.s24u)
        self.left("h", self.s24u)
        self.left("in", self.xs.at[:, 0:384])
        self.left("cot", self.og.at[0])
        self.left("far", self.cmx)
        for key in ("v4", "vz", "gz", "g4"):
            self.left(key, self.v4)
        for key in ("vy", "gy"):
            self.left(key, self.gvy)
        self.left("ig", self.out_ig.at[0:6])
        for seq in range(NSEQ):
            self.left("out%d" % seq, self.out_rows.at[0:3])


    def rows_in(self, src, dst):
        here = pl.ds(mult(self.s * BLK), BLK)
        for peer in self.speers:
            self.send(src.at[pl.ds(peer[1] * NSEQ, NSEQ)], dst.at[:, here], peer, "in", "in")
        self.in_own = self.local(src.at[pl.ds(self.s * NSEQ, NSEQ)], dst.at[:, here], 0)

    def rows_out(self, pick, dst, seq, key, number):
        there = self.s * NSEQ + seq
        for peer in self.speers:
            self.send(pick(peer[1]), dst.at[there], peer, key, key)
        self.waits.append(self.local(pick(self.s), dst.at[there], number))

    def do_igout(self):
        for seq in range(NSEQ):
            pick = lambda o, seq=seq: self.og.at[lax.div(o, 2), seq, pl.ds(mult(lax.rem(o, 2) * BLK), BLK)]
            self.rows_out(pick, self.out_ig, seq, "ig", 2 + seq)

    def do_out(self, seq):
        pick = lambda o: self.qs.at[seq, pl.ds(mult(o * BLK), BLK)]
        self.rows_out(pick, self.out_rows, seq, "out%d" % seq, 4 + seq)


    def mask_rows(self):
        other = self.xpeer[1]
        return [self.s * NSEQ + i for i in range(NSEQ)] + [other * NSEQ + i for i in range(NSEQ)]

    def cot_start(self):
        here = pl.ds(mult(self.c * BLK), BLK)
        twin = self.twin[1]
        other = lambda s: lax.rem(s + 2, 4)
        self.cot_own = []
        for half in range(2):
            mine = self.s if half == 0 else other(self.s)
            theirs = twin if half == 0 else other(twin)
            dst = self.og.at[half, :, here]
            self.cot_own.append(self.local(self.outg.at[pl.ds(mine * NSEQ, NSEQ)], dst, 6 + half))
            self.send(self.outg.at[pl.ds(theirs * NSEQ, NSEQ)], dst, self.twin, "cot", "cot")

    def do_tog(self):
        for copy in self.cot_own:
            copy.wait()
        self.arrived("cot", self.og.at[0])
        here = pl.ds(mult(self.x * 256, 256), 256)
        for i in range(NSEQ):
            rows = slice(SLOTS * i, SLOTS * (i + 1))
            self.cmx[rows] = dot(self.sel[NSEQ + i, :, here], self.og[1, i]).astype(BF)
        self.send(self.cmx, self.cmr, self.xpeer, "far", "far")

    def do_pickC(self):
        self.arrived("far", self.cmr)
        here = pl.ds(mult(self.x * 256, 256), 256)
        for i in range(NSEQ):
            rows = slice(SLOTS * i, SLOTS * (i + 1))
            near = dot(self.sel[i, :, here], self.og[0, i]).astype(BF)
            self.cm[rows] = near + self.cmr[rows]


    def view(self, arrays, name, zi, yi, xi, plane):
        w, base, h = CHUNKS[name][:3]
        if w == "d":
            return arrays[w].at[zi, yi, xi, pl.ds(mult(plane * 96, 96), 96), pl.ds(base, h)]
        return arrays[w].at[zi, yi, xi, :, pl.ds(mult(base + plane * h), h)]

    def boxed(self, arrays, name, box):
        return self.view(arrays, name, box["z"], box["y"], box["x"], self.c)

    def own_box(self):
        return {"z": pl.ds(self.z, 1), "y": pl.ds(self.y, 1), "x": pl.ds(self.x, 1)}

    def across(self, axis):
        if axis == "x":
            return [(pl.ds(1 - self.x, 1), self.xpeer)]
        if axis == "y":
            return [(pl.ds(1 - self.y, 1), self.ypeer)]
        return [(pl.ds(lax.rem(self.z + j + 1, 4), 1), self.zpeers[j]) for j in range(3)]

    def spot(self, name):
        w, base, h = CHUNKS[name][:3]
        return pl.ds(base if w == "d" else base // 2, h)


    def do_start(self):
        self.greet()
        self.waits = []
        self.rows_in(self.inp, self.xs)
        for j in range(3):
            self.send(self.vec_in, self.v4.at[j], self.speers[j], "v4", "v4")
        self.s24 = {"q": self.s24q, "o": self.s24o, "u": self.s24u}
        self.sib = {"q": self.sibq, "o": self.sibo, "u": self.sibu}
        flat = {"q": self.fq, "o": self.fo, "u": self.fu}
        self.have = set()
        for w in ("q", "o", "u"):
            n = COLS[w] // 128
            for k in range(n):
                self.s24[w][:, 128 * k : 128 * (k + 1)] = flat[w][pl.ds(k, 24, stride=n), :]
            for name, (cw, base, h, _, _) in CHUNKS.items():
                if cw == w:
                    src = self.s24[w].at[:, pl.ds(mult(base + (1 - self.c) * h), h)]
                    self.send(src, self.sib[w].at[:, self.spot(name)], self.twin, "f" + name, "f")
        for k in range(6):
            rows = pl.ds(mult(self.c * 96, 96), 96)
            self.wd[self.z, self.y, self.x, rows, 128 * k : 128 * (k + 1)] = self.fd[pl.ds(k, 96, stride=6), :].astype(BF)
        self.cot_start()
        self.sums_start()

    def own_piece(self, name):
        w, base, h = CHUNKS[name][:3]
        if w == "d":
            return
        self.arrived("f" + name, self.sib[w].at[:, self.spot(name)])
        mine = self.s24[w][:, pl.ds(mult(base + self.c * h), h)]
        theirs = self.sib[w][:, self.spot(name)]
        first = self.c == 0
        top = jnp.where(first, mine, theirs)
        bottom = jnp.where(first, theirs, mine)
        cols = pl.ds(mult(base + self.c * h), h)
        self.W[w][self.z, self.y, self.x, :, cols] = jnp.concatenate([top, bottom], axis=0).astype(BF)

    def mirror(self, name, box):
        v = self.boxed(self.W, name, box)
        self.send(v, v, self.twin, "m" + name, "m" + name)

    def do_ag(self, name, stage):
        order = CHUNKS[name][3]
        box = self.own_box()
        for axis in order[: max(stage - 1, 0)]:
            box[axis] = ALL
        if stage == 0:
            self.own_piece(name)
        else:
            axis = order[stage - 1]
            count = pl.ds(0, 3 if axis == "z" else 1)
            self.arrived((name, stage - 1), self.boxed(self.W, name, dict(box, **{axis: count})))
            if stage == 1:
                self.mirror(name, dict(box, **{axis: ALL}))
            elif axis == "z":
                for j in range(3):
                    self.mirror(name, dict(box, z=pl.ds(self.zfrom[j], 1)))
            else:
                self.mirror(name, dict(box, **{axis: self.across(axis)[0][0]}))
            box[axis] = ALL
        if stage < 3:
            v = self.boxed(self.W, name, box)
            for _, peer in self.across(order[stage]):
                self.send(v, v, peer, (name, stage), "g" + name)

    def need(self, *names):
        for name in names:
            if name not in self.have:
                self.have.add(name)
                self.arrived("m" + name, self.view(self.W, name, ALL, ALL, ALL, 1 - self.c))

    def need_weight(self, w, base=None):
        self.need(*[n for n, c in CHUNKS.items() if c[0] == w and (base is None or c[1] // D == base // D)])

    def do_vec0(self):
        self.arrived("v4", self.v4)
        self.vb[self.z, self.y] = self.vec_in[...] + self.v4[0] + self.v4[1] + self.v4[2]
        v = self.vb.at[self.z, self.y]
        for peer in self.zpeers:
            self.send(v, v, peer, "vz", "vz")

    def do_vec1(self):
        self.arrived("vz", self.v4)
        v = self.vb.at[:, self.y]
        self.send(v, v, self.ypeer, "vy", "vy")

    def do_vec(self):
        self.arrived("vy", self.gvy)
        self.load_vector()


    def sums_start(self):
        self.FIN = {"q": self.finq, "o": self.fino, "u": self.finu, "d": self.find}
        self.FR = {"q": self.frq, "o": self.fro, "u": self.fru}
        self.OUT = {"q": self.outq, "o": self.outo, "u": self.outu, "d": self.outd}

    def do_rs(self, name, stage):
        order = CHUNKS[name][4]
        if stage < 0:
            v = self.view(self.G, name, ALL, ALL, ALL, 1 - self.c)
            self.send(v, self.__dict__["rt" + name], self.twin, "t" + name, "t" + name)
            return
        if stage == 0:
            self.arrived("t" + name, self.__dict__["rt" + name])
        elif stage < 4:
            self.arrived(("s", name, stage - 1), self.__dict__["r%d" % (stage - 1) + name])
        elif CHUNKS[name][0] != "d":
            self.arrived("h" + name, self.FR[CHUNKS[name][0]].at[:, self.spot(name)])
        if stage == 4:
            self.sum_write(name)
            return
        box = {"z": ALL, "y": ALL, "x": ALL}
        own = self.own_box()
        for axis in order[:stage]:
            box[axis] = own[axis]
        if stage == 3:
            self.sum_last(name, box)
            return
        if stage == 0:
            self.add_parts(name, box, self.__dict__["rt" + name], False)
        else:
            self.add_parts(name, box, self.__dict__["r%d" % (stage - 1) + name], order[stage - 1] == "z")
        into = self.__dict__["r%d" % stage + name]
        for j, (index, peer) in enumerate(self.across(order[stage])):
            v = self.boxed(self.G, name, dict(box, **{order[stage]: index}))
            dst = into.at[pl.ds(j, 1)] if order[stage] == "z" else into
            self.send(v, dst, peer, ("s", name, stage), "s" + name)

    def add_parts(self, name, box, part, three):
        if three:
            v = self.boxed(self.G, name, box)
            total = v[...].astype(F32) + part[0:1].astype(F32)
            total = total + part[1:2].astype(F32) + part[2:3].astype(F32)
            v[...] = total.astype(BF)
        elif box["z"] is ALL:

            def body(zi, _):
                v = self.boxed(self.G, name, dict(box, z=pl.ds(zi, 1)))
                v[...] = v[...] + part[pl.ds(zi, 1)]
                return 0

            lax.fori_loop(0, 4, body, 0)
        else:
            v = self.boxed(self.G, name, box)
            v[...] = v[...] + part[...]

    def sum_last(self, name, box):
        w = CHUNKS[name][0]
        rows = 96 if w == "d" else 48
        part = self.__dict__["r2" + name]
        total = self.boxed(self.G, name, box)[...].astype(F32).reshape(rows, -1)
        for j in range(part.shape[0]):
            total = total + part[j, 0, 0].astype(F32)
        self.FIN[w][:, self.spot(name)] = total
        if w != "d":
            src = self.FIN[w].at[pl.ds(mult((1 - self.c) * 24, 8), 24), self.spot(name)]
            self.send(src, self.FR[w].at[:, self.spot(name)], self.twin, "h" + name, "h")

    def sum_write(self, name):
        w, base, h = CHUNKS[name][:3]
        n = COLS[w] // 128
        if w == "d":
            for k in range(base // 128, (base + h) // 128):
                self.outd[pl.ds(k, 96, stride=n), :] = self.find[:, 128 * k : 128 * (k + 1)]
            return
        for plane in range(2):
            for k in range(h // 128):
                lc = base // 2 + 128 * k
                own = self.FIN[w][pl.ds(mult(self.c * 24, 8), 24), lc : lc + 128]
                other = self.FR[w][:, lc : lc + 128]
                val = jnp.where(self.c == plane, own, other)
                self.OUT[w][pl.ds((base + plane * h) // 128 + k, 24, stride=n), :] = val

    def do_gv0(self):
        self.store_vector_grads()
        self.send(self.gvb.at[:, 1 - self.y], self.gvy, self.ypeer, "gy", "gy")

    def do_gv1(self):
        self.arrived("gy", self.gvy)
        for zi in range(4):
            self.gvb[zi, self.y] = self.gvb[zi, self.y] + self.gvy[zi]
        for j in range(3):
            src = self.gvb.at[lax.rem(self.z + j + 1, 4), self.y]
            self.send(src, self.gvz.at[j], self.zpeers[j], "gz", "gz")

    def do_gv2(self):
        self.arrived("gz", self.gvz)
        self.gvs[...] = self.gvb[self.z, self.y] + self.gvz[0] + self.gvz[1] + self.gvz[2]
        for j in range(3):
            self.send(self.gvs, self.gv4.at[j], self.speers[j], "g4", "g4")

    def do_gv3(self):
        self.arrived("g4", self.gv4)
        self.outv[...] = self.gvs[...] + self.gv4[0] + self.gv4[1] + self.gv4[2]


    def do_masks(self):
        self.make_masks()

    def do_pickX(self):
        self.arrived("in", self.xs.at[:, 0:384])
        self.in_own.wait()
        self.pick(self.xs, self.xm)

    def do_projK(self):
        self.need_weight("q", D)
        self.project(D, self.ks, None, False)

    def do_projV(self):
        self.need_weight("q", 2 * D)
        self.project(2 * D, self.vs, BV, False)

    def do_projQ(self):
        self.need_weight("q", 0)
        self.project(0, self.qs, BQ, True)
        self.pick(self.qs, self.qm)

    def do_att(self, part):
        step = 12 // ATT_PARTS
        self.attend(part * step, part * step + step)

    def do_branch(self):
        self.need_weight("o")
        self.pick(self.qs, self.am)
        self.marked_branch()

    def do_up(self, fb):
        self.need_weight("u", fb * D)
        self.marked_up(fb)

    def do_down(self, name):
        self.need(name)
        self.marked_down(CHUNKS[name][1], CHUNKS[name][2])

    def do_sback(self):
        self.second_back()

    def do_gd(self):
        self.grad_down()

    def do_iback(self):
        self.inner_back()

    def do_gu(self, fb):
        self.grad_up(fb)

    def do_fback(self):
        self.first_back()

    def do_go(self):
        self.grad_out()

    def do_ab(self, part):
        self.attend_back(4 * part, 4 * part + 4)

    def do_inb(self):
        self.input_back()

    def do_gq(self, name):
        if not self.released:
            self.released = True
            self.release_gather()
        self.grad_qkv(CHUNKS[name][1])

    def do_fin(self, tile):
        self.finish_rows(tile)

    def do_end(self):
        self.arrived("ig", self.out_ig.at[0:6])
        for seq in range(NSEQ):
            self.arrived("out%d" % seq, self.out_rows.at[0:3])
        for copy in self.waits:
            copy.wait()
        self.finish()


def linked_kernel(*refs):
    k = Links(dict(zip(LINKED_NAMES, refs)))
    k.do_start()
    k.do_ag(O, 0)
    k.do_ag(V, 0)
    k.do_ag(U2, 0)
    k.do_ag(U0, 0)
    k.do_ag(U1, 0)
    k.do_ag(O, 1)
    k.do_ag(K, 0)
    k.do_ag(Q, 0)
    k.do_ag(V, 1)
    k.do_ag(U1, 1)
    k.do_ag(D0, 0)
    k.do_ag(K, 1)
    k.do_ag(D1, 0)
    k.do_ag(Q, 1)
    k.do_vec0()
    k.do_ag(V, 2)
    k.do_ag(U3, 0)
    k.do_vec1()
    k.do_ag(D0, 1)
    k.do_ag(D2, 0)
    k.do_masks()
    k.do_ag(U0, 1)
    k.do_ag(D1, 1)
    k.do_ag(U2, 1)
    k.do_ag(Q, 2)
    k.do_ag(D1, 2)
    k.do_ag(V, 3)
    k.do_ag(K, 2)
    k.do_ag(D2, 1)
    k.do_ag(Q, 3)
    k.do_pickX()
    k.do_ag(U3, 1)
    k.do_vec()
    k.do_projQ()
    k.do_ag(O, 2)
    k.do_ag(D0, 2)
    k.do_ag(U2, 2)
    k.do_ag(U1, 2)
    k.do_projV()
    k.do_ag(U3, 2)
    k.do_ag(K, 3)
    k.do_projK()
    k.do_att(0)
    k.do_ag(U0, 2)
    k.do_att(1)
    k.do_att(2)
    k.do_att(3)
    k.do_att(4)
    k.do_ag(O, 3)
    k.do_ag(U1, 3)
    k.do_ag(D2, 2)
    k.do_tog()
    k.do_ag(D0, 3)
    k.do_att(5)
    k.do_branch()
    k.do_ag(U3, 3)
    k.do_ag(U0, 3)
    k.do_up(1)
    k.do_up(0)
    k.do_ag(U2, 3)
    k.do_up(3)
    k.do_ag(D1, 3)
    k.do_up(2)
    k.do_ag(D2, 3)
    k.do_down(D1)
    k.do_down(D0)
    k.do_down(D2)
    k.do_pickC()
    k.do_sback()
    k.do_gd()
    k.do_rs(D1, -1)
    k.do_rs(D2, -1)
    k.do_rs(D0, -1)
    k.do_iback()
    k.do_rs(D1, 0)
    k.do_rs(D2, 0)
    k.do_gu(3)
    k.do_rs(U3, -1)
    k.do_rs(D0, 0)
    k.do_gu(0)
    k.do_rs(U0, -1)
    k.do_fback()
    k.do_ab(0)
    k.do_rs(U0, 0)
    k.do_rs(U3, 0)
    k.do_ab(1)
    k.do_rs(D2, 1)
    k.do_rs(D0, 1)
    k.do_gu(1)
    k.do_rs(U1, -1)
    k.do_ab(2)
    k.do_rs(U0, 1)
    k.do_rs(U1, 0)
    k.do_inb()
    k.do_igout()
    k.do_gq(K)
    k.do_rs(K, -1)
    k.do_go()
    k.do_rs(U3, 1)
    k.do_rs(U0, 2)
    k.do_gq(Q)
    k.do_rs(Q, -1)
    k.do_rs(U1, 1)
    k.do_gu(2)
    k.do_rs(U2, -1)
    k.do_rs(O, -1)
    k.do_rs(D1, 1)
    k.do_rs(K, 0)
    k.do_fin(0)
    k.do_rs(U3, 2)
    k.do_rs(U2, 0)
    k.do_rs(O, 0)
    k.do_rs(Q, 0)
    k.do_fin(1)
    k.do_out(0)
    k.do_rs(K, 1)
    k.do_gq(V)
    k.do_rs(V, -1)
    k.do_fin(2)
    k.do_fin(3)
    k.do_rs(U2, 1)
    k.do_rs(D1, 2)
    k.do_rs(U1, 2)
    k.do_rs(V, 0)
    k.do_gv0()
    k.do_rs(D2, 2)
    k.do_rs(O, 1)
    k.do_rs(U2, 2)
    k.do_gv1()
    k.do_rs(K, 2)
    k.do_rs(Q, 1)
    k.do_rs(V, 1)
    k.do_rs(U0, 3)
    k.do_rs(U0, 4)
    k.do_rs(Q, 2)
    k.do_rs(U2, 3)
    k.do_gv2()
    k.do_rs(D0, 2)
    k.do_out(1)
    k.do_rs(D1, 3)
    k.do_rs(O, 2)
    k.do_rs(U1, 3)
    k.do_rs(U1, 4)
    k.do_rs(D0, 3)
    k.do_rs(Q, 3)
    k.do_rs(V, 2)
    k.do_rs(K, 3)
    k.do_rs(O, 3)
    k.do_rs(O, 4)
    k.do_gv3()
    k.do_rs(U3, 3)
    k.do_rs(U2, 4)
    k.do_rs(U3, 4)
    k.do_rs(K, 4)
    k.do_rs(V, 3)
    k.do_rs(D2, 3)
    k.do_rs(D2, 4)
    k.do_rs(V, 4)
    k.do_rs(D1, 4)
    k.do_rs(Q, 4)
    k.do_rs(D0, 4)
    k.do_end()

def plain_kernel(*refs):
    k = Layer(dict(zip(PLAIN_NAMES, refs)))
    pairs = [(k.inp, k.xs), (k.outg, k.ogl), (k.inq, k.wq), (k.ino, k.wo), (k.inu, k.wu), (k.ind, k.wd)]
    copies = [pltpu.make_async_copy(src, dst, k.lsem.at[n]) for n, (src, dst) in enumerate(pairs)]
    for copy in copies:
        copy.start()
    for copy in copies:
        copy.wait()
    k.make_masks()
    k.load_vector()
    k.pick(k.xs, k.xm)
    k.project(D, k.ks, None, False)
    k.project(2 * D, k.vs, BV, False)
    k.project(0, k.qs, BQ, True)
    k.pick(k.qs, k.qm)
    k.attend(0, 12)
    k.pick(k.qs, k.am)
    k.marked_branch()
    for fb in range(4):
        k.marked_up(fb)
    k.pick(k.ogl, k.cm)
    for first in (0, 256, 512):
        k.marked_down(first, 256)
    k.second_back()
    k.grad_down()
    k.inner_back()
    for fb in range(4):
        k.grad_up(fb)
    k.first_back()
    k.grad_out()
    k.attend_back(0, 12)
    k.input_back()
    k.store_vector_grads()
    for first in (D, 2 * D, 0):
        k.grad_qkv(first)
    for tile in range(4):
        k.finish_rows(tile)
    for seq in range(NSEQ):
        for half in range(2):
            k.ogl[seq, 256 * half : 256 * half + 256] = k.og[half, seq]
    pairs = [(k.qs, k.out_rows), (k.ogl, k.out_ig), (k.wq, k.outq), (k.go, k.outo), (k.gu, k.outu), (k.gd, k.outd)]
    copies = [pltpu.make_async_copy(src, dst, k.lsem.at[n]) for n, (src, dst) in enumerate(pairs)]
    for copy in copies:
        copy.start()
    for copy in copies:
        copy.wait()
    k.outv[...] = k.gvb[...]


def wshape(w):
    return (4, 2, 2, PIECE[w], COLS[w])


COMMON_SCRATCH = [
    ("wq", wshape("q"), BF),
    ("wo", wshape("o"), BF),
    ("wu", wshape("u"), BF),
    ("wd", wshape("d"), BF),
    ("xs", (NSEQ, LEN, D), BF),
    ("og", (2, NSEQ, 256, D), BF),
    ("qs", (NSEQ, LEN, D), BF),
    ("ks", (NSEQ, LEN, D), BF),
    ("vs", (NSEQ, LEN, D), BF),
    ("sel", (2 * NSEQ, SLOTS, LEN), BF),
    ("kmask", (NSEQ, LEN, 128), BF),
    ("vrow", (1, VEC), F32),
    ("gvrow", (1, VEC), F32),
    ("gvb", (4, 2, 16, 128), F32),
    ("xm", (MROWS, D), BF),
    ("am", (MROWS, D), BF),
    ("qm", (MROWS, D), BF),
    ("cm", (MROWS, D), BF),
    ("low", (MROWS, D), BF),
    ("g2", (MROWS, D), BF),
    ("ga", (MROWS, D), BF),
    ("gq", (MROWS, D), BF),
    ("f0", (MROWS, D), F32),
    ("f1", (MROWS, D), F32),
    ("f3", (MROWS, D), F32),
    ("sc1", (MROWS, 128), F32),
    ("act", (MROWS, FF), BF),
    ("dgl", (MROWS, FF), F32),
    ("gd", wshape("d"), BF),
    ("gu", wshape("u"), BF),
    ("go", wshape("o"), BF),
    ("tlow", (256, D), BF),
    ("tacc", (256, D), F32),
]


def linked_scratch():
    out = list(COMMON_SCRATCH)
    out += [("vb", (4, 2, 16, 128), F32), ("v4", (3, 16, 128), F32)]
    for w in ("q", "o", "u"):
        out += [("s24" + w, (24, COLS[w]), F32), ("sib" + w, (24, COLS[w] // 2), F32)]
    for w in ("q", "o", "u", "d"):
        rows = 96 if w == "d" else 48
        half = D if w == "d" else COLS[w] // 2
        out.append(("fin" + w, (rows, half), F32))
        if w != "d":
            out.append(("fr" + w, (24, half), F32))
    for name, (w, _, h, _, order) in CHUNKS.items():
        rows = 96 if w == "d" else 48
        shape = dict(FULL)
        out.append(("rt" + name, (4, 2, 2, rows, h), BF))
        for stage, axis in enumerate(order):
            shape[axis] = 3 if axis == "z" else 1
            out.append(("r%d" % stage + name, (shape["z"], shape["y"], shape["x"], rows, h), BF))
            shape[axis] = 1
    out += [
        ("cmx", (MROWS, D), BF),
        ("cmr", (MROWS, D), BF),
        ("gvy", (4, 16, 128), F32),
        ("gvz", (3, 16, 128), F32),
        ("gvs", (16, 128), F32),
        ("gv4", (3, 16, 128), F32),
    ]
    return out


LINKED_SCRATCH = linked_scratch()
LINKED_INS = ["lengths", "spans", "inp", "outg", "fq", "fo", "fu", "fd", "vec_in"]
LINKED_OUTS = ["out_rows", "out_ig", "outq", "outo", "outu", "outd", "outv"]
LINKED_NAMES = LINKED_INS + LINKED_OUTS + [n for n, _, _ in LINKED_SCRATCH] + ["ssem", "rsem", "lsem"]
PLAIN_INS = ["lengths", "spans", "inp", "outg", "inq", "ino", "inu", "ind", "vb"]
PLAIN_SCRATCH = COMMON_SCRATCH + [("ogl", (NSEQ, LEN, D), BF)]
PLAIN_NAMES = PLAIN_INS + LINKED_OUTS + [n for n, _, _ in PLAIN_SCRATCH] + ["lsem"]

IN_VMEM = pl.BlockSpec(memory_space=pltpu.VMEM)
IN_SMEM = pl.BlockSpec(memory_space=pltpu.SMEM)
ANYWHERE = pl.BlockSpec(memory_space=pl.ANY)


def flat_shape(w):
    return (OWN_ROWS[w] * COLS[w] // 128, 128)


def linked_call(lengths, spans, inp, outg, flats, vec_in):
    outs = [jax.ShapeDtypeStruct((8, BLK, D), BF)] * 2
    outs += [jax.ShapeDtypeStruct(flat_shape(w), F32) for w in ("q", "o", "u", "d")]
    outs += [jax.ShapeDtypeStruct((16, 128), F32)]
    return pl.pallas_call(
        linked_kernel,
        out_shape=outs,
        in_specs=[IN_SMEM, IN_VMEM, ANYWHERE, ANYWHERE] + [IN_VMEM] * 5,
        out_specs=[ANYWHERE, ANYWHERE] + [IN_VMEM] * 5,
        scratch_shapes=[pltpu.VMEM(shape, dtype) for _, shape, dtype in LINKED_SCRATCH]
        + [pltpu.SemaphoreType.DMA((NSEND,)), pltpu.SemaphoreType.DMA((NRECV,)), pltpu.SemaphoreType.DMA((8,))],
        compiler_params=pltpu.CompilerParams(
            collective_id=0, has_side_effects=True, vmem_limit_bytes=64 * 2**20 - 2**16
        ),
        name="layer",
    )(lengths, spans, inp, outg, *flats, vec_in)


def plain_call(lengths, spans, inp, outg, weights, vb):
    outs = [jax.ShapeDtypeStruct((NSEQ, LEN, D), BF)] * 2
    outs += [jax.ShapeDtypeStruct(wshape(w), BF) for w in ("q", "o", "u", "d")]
    outs += [jax.ShapeDtypeStruct((4, 2, 16, 128), F32)]
    return pl.pallas_call(
        plain_kernel,
        out_shape=outs,
        in_specs=[IN_SMEM, IN_VMEM] + [ANYWHERE] * 6 + [IN_VMEM],
        out_specs=[ANYWHERE] * 6 + [IN_VMEM],
        scratch_shapes=[pltpu.VMEM(shape, dtype) for _, shape, dtype in PLAIN_SCRATCH]
        + [pltpu.SemaphoreType.DMA((8,))],
        compiler_params=pltpu.CompilerParams(vmem_limit_bytes=60 * 2**20),
        name="layer",
    )(lengths, spans, inp, outg, *weights, vb)


def adam_update(master, first_moment, second_moment, gradient, step_rate, decay_rate):
    new_first = FIRST_DECAY * first_moment + (1.0 - FIRST_DECAY) * gradient
    new_second = SECOND_DECAY * second_moment + (1.0 - SECOND_DECAY) * gradient * gradient
    first_hat = new_first / (1.0 - FIRST_DECAY**STEP)
    second_hat = new_second / (1.0 - SECOND_DECAY**STEP)
    new_master = master - step_rate * (
        first_hat / (jnp.sqrt(second_hat) + ADAM_EPS) + decay_rate * master
    )
    return (new_master, new_first, new_second, new_master.astype(jnp.bfloat16))


RATES = (1.6 / math.sqrt(D), 1.6 / math.sqrt(D), 1.6 / math.sqrt(D), 1.6 / math.sqrt(FF))


def adam_kernel(*refs):
    for n in range(4):
        grad, master, first, second = (refs[4 * n + m][...] for m in range(4))
        for out, value in zip(refs[16 + 4 * n : 20 + 4 * n], adam_update(master, first, second, grad, RATES[n], 0.01)):
            out[...] = value


def adam_call(groups):
    steps = 3
    specs, outs, out_specs, flat = [], [], [], []
    for group in groups:
        rows = group[0].shape[0]
        spec = pl.BlockSpec((rows // steps, 128), lambda i: (i, 0))
        specs += [spec] * 4
        out_specs += [spec] * 4
        outs += [jax.ShapeDtypeStruct((rows, 128), F32)] * 3 + [jax.ShapeDtypeStruct((rows, 128), BF)]
        flat += list(group)
    new = pl.pallas_call(
        adam_kernel,
        out_shape=outs,
        grid=(steps,),
        in_specs=specs,
        out_specs=out_specs,
        compiler_params=pltpu.CompilerParams(vmem_limit_bytes=32 * 2**20),
        name="adam",
    )(*flat)
    return [tuple(a.reshape(-1) for a in new[4 * n : 4 * n + 4]) for n in range(4)]


def on_device(
    inputs,
    out_grad,
    lengths,
    word_spans,
    qkv_weight,
    qkv_first,
    qkv_second,
    out_weight,
    out_first,
    out_second,
    up_weight,
    up_first,
    up_second,
    down_weight,
    down_first,
    down_second,
    vec_weight,
    vec_first,
    vec_second,
):
    groups = [
        (qkv_weight, qkv_first, qkv_second),
        (out_weight, out_first, out_second),
        (up_weight, up_first, up_second),
        (down_weight, down_first, down_second),
    ]
    everywhere = ("batch", "seq")
    if lax.axis_size("batch") == 8 and lax.axis_size("seq") == 4:
        place = lax.axis_index("seq")
        share = vec_weight.shape[0]
        vec_in = lax.dynamic_update_slice(jnp.zeros((16 * 128,), F32), vec_weight, (share * place,)).reshape(16, 128)
        flats = [group[0].reshape(-1, 128) for group in groups]
        rows, in_grad, *sums, vec_sum = linked_call(lengths, word_spans, inputs, out_grad, flats, vec_in)
        vec_grad = lax.dynamic_slice(vec_sum.reshape(-1), (share * place,), (share,))
        news = adam_call([(g,) + tuple(a.reshape(-1, 128) for a in group) for g, group in zip(sums, groups)])
        in_grad = in_grad.astype(F32)
    else:
        weights = [
            lax.all_gather(group[0].astype(BF), everywhere, axis=0, tiled=True).reshape(wshape(w))
            for w, group in zip("qoud", groups)
        ]
        vector = lax.all_gather(vec_weight.astype(BF), everywhere, axis=0, tiled=True).astype(F32)
        vb = jnp.pad(vector.reshape(4, 2, VROWS, 128), ((0, 0), (0, 0), (0, 16 - VROWS), (0, 0)))
        own = lax.axis_index("seq") * NSEQ
        xs, og = (
            lax.all_to_all(a, "seq", split_axis=0, concat_axis=1, tiled=True) for a in (inputs, out_grad)
        )
        rows, in_grad, *grads, gvb = plain_call(lengths, word_spans, xs, og, weights, vb)
        rows, in_grad = (
            lax.all_to_all(a, "seq", split_axis=1, concat_axis=0, tiled=True) for a in (rows, in_grad)
        )
        in_grad = in_grad.astype(F32)
        sums = [
            lax.psum_scatter(g.astype(F32).reshape(-1), everywhere, scatter_dimension=0, tiled=True) for g in grads
        ]
        vec_grad = lax.psum_scatter(
            gvb[:, :, :VROWS].reshape(-1), everywhere, scatter_dimension=0, tiled=True
        )
        news = [
            adam_update(master, first, second, g, rate, 0.01)
            for (master, first, second), g, rate in zip(groups, sums, RATES)
        ]
    vec_new = adam_update(vec_weight, vec_first, vec_second, vec_grad, 0.4, 0.0)
    flat = [array for new in news for array in new]
    return (rows, in_grad, *flat, *vec_new)


def solution(mesh):
    owned = P(("batch", "seq"))
    rows = P("batch", "seq", None)
    in_specs = (rows, rows, P("batch"), P("batch", None, None)) + (owned,) * 15
    out_specs = (rows, rows) + (owned,) * 20
    return jax.shard_map(on_device, mesh=mesh, in_specs=in_specs, out_specs=out_specs, check_vma=False)
```
